32 devices in a mesh: space: 16 (over z, y, core), snap: 2 (over x).
Axes of the slice: x: 2, y: 2, z: 4, core: 2. Of those that a mesh axis runs over, the one named last changes fastest.
Arguments:
- forcing_direct: bfloat16 [1024, 16, 16, 128], P('snap', 'space'), may hold values from -6 to 6
- forcing_adjoint: bfloat16 [1024, 16, 16, 128], P('snap', 'space'), may hold values from -6 to 6
- conductance: float32 [16, 16, 128], P('space'), may hold values from 0.25 to 4
- shift_table: float32 [16], replicated, may hold values from 0.2 to 3
- freq_direct: int32 [1024], P('snap'), may hold values from 0 to 15
- freq_adjoint: int32 [1024], P('snap'), may hold values from 0 to 15
- left_factors: float32 [1024, 64], replicated, may hold values from -0.1875 to 0.1875
- right_factors: float32 [1024, 64], replicated, may hold values from -0.1875 to 0.1875
- singular_values: float32 [64], replicated, may hold values from 0.25 to 4
Outputs:
- gram: float32 [1024, 1024], P('snap', 'space')
- direct_modes: float32 [64, 16, 16, 128], P(None, 'space', 'snap')
- adjoint_modes: float32 [64, 16, 16, 128], P(None, 'space', 'snap')
The draws below stay inside these ranges and needn't reach their ends.
All inputs are finite; a program needn't handle non-finite values.
Results may differ from the reference program's by a relative error of at most 0.0041.
Values may be sent and summed in bfloat16 or wider, within the bound.
No kernel may reach another device: no remote copies, remote signals or barrier semaphores. Data moves between devices by JAX's collectives and lax.ppermute only.
A program may use at most 128 MiB of HBM per device.

```python
import math
import jax
import jax.numpy as jnp
from jax import lax

NS = 1024
R = 64
NF = 16
GY = 16
GZ = 128
NX = 16


def set_ends(values, stream_key, least, largest):
    dims = values.shape
    spot = [jax.random.randint(jax.random.fold_in(stream_key, axis), (), 0, dims[axis]) for axis in range(len(dims))]
    values = values.at[tuple(spot)].set(least)
    longest = dims.index(max(dims))
    spot[longest] = (spot[longest] + 1) % dims[longest]
    return values.at[tuple(spot)].set(largest)


def level_of(own_key, dims, cuts, low, high):
    gain = 1.0
    for position, parts in cuts:
        steps = jax.random.uniform(jax.random.fold_in(jax.random.fold_in(own_key, 6), position), (parts,), jnp.float32, low / len(cuts), high / len(cuts))
        gain = gain * jnp.repeat(jnp.exp(steps), dims[position] // parts).reshape((-1,) + (1,) * (len(dims) - 1 - position))
    return gain


def noise(own_key, dims, width, reach, cuts=(), kind=jnp.bfloat16):
    entries = jax.random.normal(own_key, dims, jnp.float32) * width
    if len(cuts) > 0:
        entries = level_of(own_key, dims, cuts, -0.22, 0.18) * entries
    return jnp.clip(entries, min=-reach, max=reach).astype(kind)


def setup_inputs(seed: int = 0) -> dict:
    arg_keys = jax.random.split(jax.random.key(seed), 10)
    return {
        "forcing_direct": noise(arg_keys[0], (NS, NX, GY, GZ), 1.0, 6.0, ((0, 2), (1, 16))),
        "forcing_adjoint": noise(arg_keys[1], (NS, NX, GY, GZ), 1.0, 6.0, ((0, 2), (1, 16))),
        "conductance": jnp.clip(jnp.exp(math.log(4.0) - 2.7725887 * jax.random.uniform(arg_keys[2], (NX, GY, GZ), jnp.float32) ** level_of(arg_keys[2], (NX, GY, GZ), ((0, 16),), -0.2, 0.2)), 0.25, 4.0),
        "shift_table": jnp.clip(jnp.exp(jax.random.uniform(arg_keys[3], (NF,), jnp.float32, math.log(0.2), math.log(3.0))), 0.2, 3.0),
        "freq_direct": set_ends(jax.random.randint(arg_keys[4], (NS,), 0, NF), jax.random.fold_in(arg_keys[4], 1), 0, NF - 1).astype(jnp.int32),
        "freq_adjoint": set_ends(jax.random.randint(arg_keys[5], (NS,), 0, NF), jax.random.fold_in(arg_keys[5], 1), 0, NF - 1).astype(jnp.int32),
        "left_factors": noise(arg_keys[6], (NS, R), NS ** -0.5, 0.1875, (), jnp.float32),
        "right_factors": noise(arg_keys[7], (NS, R), NS ** -0.5, 0.1875, (), jnp.float32),
        "singular_values": jnp.clip(jnp.exp(jax.random.uniform(arg_keys[8], (R,), jnp.float32, math.log(0.25), math.log(4.0))), 0.25, 4.0),
    }


def lookup(indices, shift_list):
    levels = jnp.arange(shift_list.shape[0], dtype=jnp.int32)
    picked = jnp.where(indices[:, None] == levels[None, :], shift_list[None, :], jnp.float32(0.0))
    return lax.optimization_barrier(jnp.sum(picked, axis=1))

def neighbours(values):
    padded = jnp.pad(values, ((0, 0), (1, 1), (1, 1), (1, 1)))
    summed = padded[:, 2:, 1:-1, 1:-1] + padded[:, :-2, 1:-1, 1:-1]
    summed = summed + padded[:, 1:-1, 2:, 1:-1] + padded[:, 1:-1, :-2, 1:-1]
    return summed + padded[:, 1:-1, 1:-1, 2:] + padded[:, 1:-1, 1:-1, :-2]

def sweeps(direct_force, adjoint_force, direct_shift, adjoint_shift, conductance):
    coeff = conductance[None]
    direct_diag = direct_shift[:, None, None, None] + 6.0 * coeff
    adjoint_diag = adjoint_shift[:, None, None, None] + 6.0 * coeff
    force_dir = direct_force.astype(jnp.float32)
    force_adj = adjoint_force.astype(jnp.float32)
    state_dir = force_dir / direct_diag
    state_adj = force_adj / adjoint_diag
    for repeat in range(2):
        state_dir = (force_dir + coeff * neighbours(state_dir)) / direct_diag
        state_adj = (force_adj + neighbours(coeff * state_adj)) / adjoint_diag
    return (state_dir.astype(jnp.bfloat16), state_adj.astype(jnp.bfloat16))

def reference(forcing_direct, forcing_adjoint, conductance, shift_table, freq_direct, freq_adjoint, left_factors, right_factors, singular_values):
    block_rows = math.gcd(NS, 128)
    blocks_count = NS // block_rows
    shift_dir = lookup(freq_direct, shift_table)
    shift_adj = lookup(freq_adjoint, shift_table)

    def one_block(pieces):
        return sweeps(pieces[0], pieces[1], pieces[2], pieces[3], conductance)
    direct, adjoint = lax.map(one_block, (forcing_direct.reshape(blocks_count, block_rows, NX, GY, GZ), forcing_adjoint.reshape(blocks_count, block_rows, NX, GY, GZ), shift_dir.reshape(blocks_count, block_rows), shift_adj.reshape(blocks_count, block_rows)))
    direct = direct.reshape(NS, NX * GY * GZ)
    adjoint = adjoint.reshape(NS, NX * GY * GZ)
    weight = 1.0 / math.sqrt(NX * GY * GZ)
    gram = jnp.dot(adjoint, direct.T, preferred_element_type=jnp.float32) * weight
    inv_root = 1.0 / jnp.sqrt(singular_values)
    right_scaled = (right_factors * inv_root[None, :]).astype(jnp.bfloat16)
    left_scaled = (left_factors * inv_root[None, :]).astype(jnp.bfloat16)
    direct_modes = jnp.dot(right_scaled.T, direct, preferred_element_type=jnp.float32).reshape(R, NX, GY, GZ)
    adjoint_modes = jnp.dot(left_scaled.T, adjoint, preferred_element_type=jnp.float32).reshape(R, NX, GY, GZ)
    return (gram, direct_modes, adjoint_modes)
```

```python
import functools
import math

import jax
import jax.numpy as jnp
from jax import lax
from jax.experimental import pallas as pl
from jax.experimental.pallas import tpu as pltpu
from jax.sharding import PartitionSpec as P

GROUP = 4
HALO = 2
STEP = 16
CHUNKS = (4, 2, 2)


def along_z(row):
    width = row.shape[-1]
    lane = lax.broadcasted_iota(jnp.int32, row.shape, 1)
    left = jnp.where(lane == 0, 0.0, pltpu.roll(row, 1, axis=1))
    right = jnp.where(lane == width - 1, 0.0, pltpu.roll(row, width - 1, axis=1))
    return left + right


def relaxed(start, gain, old, plane, y, width_y):
    row = old[plane, y]
    total = old[plane - 1, y] + old[plane + 1, y]
    if y > 0:
        total = total + old[plane, y - 1]
    if y < width_y - 1:
        total = total + old[plane, y + 1]
    total = total + along_z(row)
    return start[plane, y] + gain[plane, y] * total


def sweep_kernel(adjoint, place, mine, theirs, early, late, shift, cond, *rest):
    if adjoint:
        inverse, out, start, gain, first = rest
    else:
        out, start, gain, first = rest
    width_y = cond.shape[1]
    level = shift[...]
    for number, source in enumerate((mine, theirs, early, late)):
        for half in range(2):
            plane = place[2 * number + half]
            for y in range(width_y):
                coeff = cond[plane, pl.ds(y, 1), :]
                diag = level + 6.0 * coeff
                guess = pl.reciprocal(diag, approx=True)
                recip = guess * (2.0 - diag * guess)
                scaled = recip * coeff
                force = source[half, y].astype(jnp.float32)
                gain[plane, y] = scaled
                start[plane, y] = force * (scaled if adjoint else recip)
    planes = GROUP + 2 * HALO
    for plane in range(1, planes - 1):
        for y in range(width_y):
            first[plane, y] = relaxed(start, gain, start, plane, y, width_y)
    for plane in range(HALO, planes - HALO):
        for y in range(width_y):
            state = relaxed(start, gain, first, plane, y, width_y)
            if adjoint:
                state = state * inverse[plane - HALO, pl.ds(y, 1), :]
            out[plane - HALO, y] = state.astype(jnp.bfloat16)


def sweep(adjoint, place, mine, theirs, early, late, shift, cond, inverse):
    _, width_y, count, width_z = mine.shape
    planes = GROUP + 2 * HALO
    pair = pl.BlockSpec((2, width_y, STEP, width_z), lambda i, *_: (0, 0, i, 0))
    whole = lambda array: pl.BlockSpec(array.shape, lambda i, *_: (0,) * array.ndim)
    fields = [cond] + ([inverse] if adjoint else [])
    scratch = pltpu.VMEM((planes, width_y, STEP, width_z), jnp.float32)
    rows = count * planes * width_y * width_z
    return pl.pallas_call(
        functools.partial(sweep_kernel, adjoint),
        grid_spec=pltpu.PrefetchScalarGridSpec(
            num_scalar_prefetch=1,
            grid=(count // STEP,),
            in_specs=[pair] * 4
            + [pl.BlockSpec((STEP, width_z), lambda i, *_: (i, 0))]
            + [whole(f) for f in fields],
            out_specs=pl.BlockSpec((GROUP, width_y, STEP, width_z), lambda i, *_: (0, 0, i, 0)),
            scratch_shapes=[scratch] * 3,
        ),
        out_shape=jax.ShapeDtypeStruct((GROUP, width_y, count, width_z), jnp.bfloat16),
        compiler_params=pltpu.CompilerParams(vmem_limit_bytes=24 * 1024 * 1024),
        cost_estimate=pl.CostEstimate(flops=40 * rows, bytes_accessed=6 * rows, transcendentals=rows),
        name="adjoint_sweeps" if adjoint else "direct_sweeps",
    )(place, mine, theirs, early, late, shift, *fields)


def gram_kernel(parts, blocks, where, own, other, left_own, left_other, *rest):
    direct = rest[:parts]
    pieces, modes, sums = rest[parts:]
    plane = pl.program_id(0)
    width_y, half = own.shape[1], own.shape[2]
    mode_count = left_own.shape[0]

    @pl.when(plane == 0)
    def _():
        sums[...] = jnp.zeros_like(sums)

    dims = (((1,), (1,)), ((), ()))
    for y in range(0, width_y, 2):
        adj = [jnp.concatenate([a[0, y], a[0, y + 1]], axis=1) for a in (own, other)]
        for part in range(parts):
            cols = jnp.concatenate([direct[part][0, y], direct[part][0, y + 1]], axis=1)
            for side in range(2):
                sums[side, part] += lax.dot_general(
                    adj[side], cols, dims, preferred_element_type=jnp.float32
                )

    @pl.when(plane == where[0])
    def _():
        for y in range(width_y):
            modes[y] = jnp.dot(
                left_own[...], own[0, y], preferred_element_type=jnp.float32
            ) + jnp.dot(left_other[...], other[0, y], preferred_element_type=jnp.float32)

    @pl.when(plane == pl.num_programs(0) - 1)
    def _():
        width = pieces.shape[2]
        for side in range(2):
            spot = pl.multiple_of(jnp.where(side == 0, where[1], 1 - where[1]) * half, half)
            for part in range(parts):
                for block in range(blocks):
                    pieces[part * blocks + block, pl.ds(spot, half), :] = sums[
                        side, part, :, block * width : (block + 1) * width
                    ]


def gram_part(where, own, other, left_own, left_other, direct, blocks):
    parts = len(direct)
    planes, width_y, half, width_z = own.shape
    cols = direct[0].shape[2]
    mode_count = left_own.shape[0]
    slab = lambda count: pl.BlockSpec((1, width_y, count, width_z), lambda p, *_: (p, 0, 0, 0))
    whole = lambda shape: pl.BlockSpec(shape, lambda p, *_: (0,) * len(shape))
    pieces = (parts * blocks, 2 * half, cols // blocks)
    modes = (width_y, mode_count, width_z)
    macs = 2 * half * cols * parts * planes * width_y * width_z
    return pl.pallas_call(
        functools.partial(gram_kernel, parts, blocks),
        grid_spec=pltpu.PrefetchScalarGridSpec(
            num_scalar_prefetch=1,
            grid=(planes,),
            in_specs=[slab(half)] * 2 + [whole(left_own.shape)] * 2 + [slab(cols)] * parts,
            out_specs=[whole(pieces), whole(modes)],
            scratch_shapes=[pltpu.VMEM((2, parts, half, cols), jnp.float32)],
        ),
        out_shape=[
            jax.ShapeDtypeStruct(pieces, jnp.float32),
            jax.ShapeDtypeStruct(modes, jnp.float32),
        ],
        compiler_params=pltpu.CompilerParams(vmem_limit_bytes=24 * 1024 * 1024),
        cost_estimate=pl.CostEstimate(
            flops=4 * macs, bytes_accessed=2 * planes * width_y * width_z * (2 * half + cols * parts), transcendentals=0
        ),
        name="gram_part",
    )(where, own, other, left_own, left_other, *direct)


def modes_kernel(parts, where, right, *rest):
    direct, out = rest[:parts], rest[parts]
    for y in range(out.shape[1]):
        out[0, y] = sum(
            jnp.dot(right[part], direct[part][0, y], preferred_element_type=jnp.float32)
            for part in range(parts)
        )


def direct_part(where, right, direct, shares):
    parts = len(direct)
    planes, width_y, cols, width_z = direct[0].shape
    mode_count = right.shape[1]
    rows_y = width_y // shares
    slab = pl.BlockSpec((1, rows_y, cols, width_z), lambda p, w: (p, w[0], 0, 0))
    return pl.pallas_call(
        functools.partial(modes_kernel, parts),
        grid_spec=pltpu.PrefetchScalarGridSpec(
            num_scalar_prefetch=1,
            grid=(planes,),
            in_specs=[pl.BlockSpec(right.shape, lambda p, w: (0, 0, 0))] + [slab] * parts,
            out_specs=pl.BlockSpec((1, rows_y, mode_count, width_z), lambda p, w: (p, 0, 0, 0)),
        ),
        out_shape=jax.ShapeDtypeStruct((planes, rows_y, mode_count, width_z), jnp.float32),
        compiler_params=pltpu.CompilerParams(vmem_limit_bytes=24 * 1024 * 1024),
        cost_estimate=pl.CostEstimate(
            flops=4 * mode_count * cols * parts * planes * rows_y * width_z,
            bytes_accessed=2 * planes * rows_y * width_z * cols * parts,
            transcendentals=0,
        ),
        name="direct_modes_part",
    )(where, right, *direct)


def lookup(indices, shift_list):
    levels = jnp.arange(shift_list.shape[0], dtype=jnp.int32)
    picked = jnp.where(indices[:, None] == levels[None, :], shift_list[None, :], jnp.float32(0.0))
    return jnp.sum(picked, axis=1)


def pick(array, index, axis=0):
    return lax.dynamic_index_in_dim(array, index, axis, keepdims=False)


def per_device(
    forcing_direct,
    forcing_adjoint,
    conductance,
    shift_table,
    freq_direct,
    freq_adjoint,
    left_factors,
    right_factors,
    singular_values,
):
    n_space, n_snap = lax.axis_size("space"), lax.axis_size("snap")
    rows, plane_x, width_y, width_z = forcing_direct.shape
    total = rows * n_snap
    layers = n_space // GROUP
    block = total // n_space
    blocks = rows // (GROUP * block)
    mode_count = left_factors.shape[1]
    rows_y = width_y // n_snap
    weight = 1.0 / math.sqrt(plane_x * n_space * width_y * width_z)

    spot, share = lax.axis_index("space"), lax.axis_index("snap")
    layer, member = spot // GROUP, spot % GROUP
    core, high = member % 2, member // 2

    def swap(array, mask):
        return lax.ppermute(array, "space", [(i, i ^ mask) for i in range(n_space)])

    ups = [(i, i + GROUP) for i in range(n_space - GROUP)]
    downs = [(i + GROUP, i) for i in range(n_space - GROUP)]
    upper = lambda pairs, wanted: [p for p in pairs if (p[0] % GROUP) // 2 == wanted]
    early_pairs = upper(ups, 1) + upper(downs, 0)
    late_pairs = upper(ups, 0) + upper(downs, 1)

    direct_blocks = forcing_direct.reshape(blocks, GROUP, block, width_y, width_z)

    def direct_set(index):
        piece = pick(direct_blocks, index, 1).reshape(blocks * block, width_y, width_z)
        return piece.transpose(1, 0, 2)

    dir_theirs = jnp.stack(
        [swap(direct_set(member ^ 2), 2), swap(direct_set(member ^ 3), 3)]
    )
    dir_mine = jnp.stack([direct_set(member), swap(direct_set(member ^ 1), 1)])

    sizes = [rows * part // sum(CHUNKS) // 2 for part in CHUNKS]
    starts = [2 * sum(sizes[:i]) for i in range(len(sizes))]

    def halves(array, index):
        kept = [
            pick(array[at : at + 2 * size].reshape((2, size) + array.shape[1:]), index)
            for at, size in zip(starts, sizes)
        ]
        return jnp.concatenate(kept, axis=0)

    adj_flat = forcing_adjoint.reshape(rows, width_y, width_z)
    adj_own = halves(adj_flat, core).transpose(1, 0, 2)
    adj_far = swap(halves(adj_flat, 1 - core).transpose(1, 0, 2), 1)
    offsets = [sum(sizes[:i]) for i in range(len(sizes))]
    adj_mine = [
        jnp.stack([adj_own[:, at : at + size], adj_far[:, at : at + size]])
        for at, size in zip(offsets, sizes)
    ]
    adj_theirs = [swap(array, 2) for array in adj_mine]

    everywhere = lax.all_gather(conductance, "space", axis=0, tiled=True)
    edge = jnp.zeros((HALO, width_y, width_z), jnp.float32)
    cond = lax.dynamic_slice_in_dim(
        jnp.concatenate([edge, everywhere, edge]), layer * GROUP, GROUP + 2 * HALO, 0
    )
    inverse = 1.0 / cond[HALO:-HALO]
    wide = lambda values: jnp.broadcast_to(values[:, None], (values.shape[0], width_z))
    dir_levels = lookup(freq_direct, shift_table).reshape(blocks, GROUP, block)
    dir_shift = wide(pick(dir_levels, member, 1).reshape(-1))
    adj_shift = wide(halves(lookup(freq_adjoint, shift_table), core))

    inside = lambda index: HALO + index
    below = lambda index: index - HALO
    above = lambda index: index + GROUP + HALO
    place = jnp.stack(
        [inside(member ^ k) for k in range(4)]
        + [jnp.where(high == 1, below(member ^ k), above(member ^ k)) for k in (0, 1)]
        + [jnp.where(high == 1, above(member ^ k), below(member ^ k)) for k in (2, 3)]
    ).astype(jnp.int32)

    def states(adjoint, mine, theirs, shift):
        early = lax.ppermute(mine, "space", early_pairs)
        late = lax.ppermute(theirs, "space", late_pairs)
        return sweep(adjoint, place, mine, theirs, early, late, shift, cond, inverse)

    dir_state = states(False, dir_mine, dir_theirs, dir_shift)
    around = lambda array, step: lax.ppermute(
        array, "snap", [(i, (i + step) % n_snap) for i in range(n_snap)]
    )
    direct = [dir_state] + [around(dir_state, step) for step in range(1, n_snap)]

    inv_root = 1.0 / jnp.sqrt(singular_values)
    right_scaled = (right_factors * inv_root[None, :]).astype(jnp.bfloat16)
    left_scaled = (left_factors * inv_root[None, :]).astype(jnp.bfloat16)
    right_sets = pick(
        right_scaled.reshape(n_snap, blocks, GROUP, block, mode_count), member, 2
    ).reshape(n_snap, blocks * block, mode_count)
    right_sets = right_sets.transpose(0, 2, 1)
    right_near = jnp.stack(
        [pick(right_sets, (share - step) % n_snap) for step in range(n_snap)]
    )
    dir_term = direct_part(share.reshape(1).astype(jnp.int32), right_near, direct, n_snap)
    dir_modes = pick(dir_term, member)
    for mask in range(1, GROUP):
        sent = pick(dir_term, member ^ mask).astype(jnp.bfloat16)
        dir_modes = dir_modes + swap(sent, mask).astype(jnp.float32)
    direct_modes = dir_modes.transpose(1, 0, 2)[:, None]

    where = jnp.stack([member, core]).astype(jnp.int32)
    left_mine = lax.dynamic_slice_in_dim(left_scaled, share * rows, rows, 0)
    left_own, left_far = halves(left_mine, core).T, halves(left_mine, 1 - core).T
    gram_rows, adj_term = [], 0.0
    for at, size, mine, theirs in zip(offsets, sizes, adj_mine, adj_theirs):
        own = states(True, mine, theirs, adj_shift[at : at + size])
        far = swap(own, 1)
        pieces, term = gram_part(
            where, own, far, left_own[:, at : at + size], left_far[:, at : at + size], direct, blocks
        )
        adj_term = adj_term + term

        def piece_for(target):
            owner, number = target // blocks, target % blocks
            return pick(pieces, ((share - owner) % n_snap) * blocks + number)

        summed = piece_for(layer)
        for step in range(1, layers):
            sent = piece_for((layer + step) % layers).astype(jnp.bfloat16)
            pairs = [(i, (i + GROUP * step) % n_space) for i in range(n_space)]
            summed = summed + lax.ppermute(sent, "space", pairs).astype(jnp.float32)
        gram_rows.append(summed * weight)
    gram = jnp.concatenate(gram_rows, axis=0)

    adj_shares = adj_term.reshape(n_snap, rows_y, mode_count, width_z)
    adj_modes = pick(adj_shares, share)
    for step in range(1, n_snap):
        sent = pick(adj_shares, (share + step) % n_snap).astype(jnp.bfloat16)
        adj_modes = adj_modes + around(sent, step).astype(jnp.float32)
    adjoint_modes = adj_modes.transpose(1, 0, 2)[:, None]
    return (gram, direct_modes, adjoint_modes)


def solution(mesh):
    placed = (
        P("snap", "space", None, None),
        P("snap", "space", None, None),
        P("space", None, None),
        P(),
        P("snap"),
        P("snap"),
        P(),
        P(),
        P(),
    )
    return jax.shard_map(
        per_device,
        mesh=mesh,
        in_specs=placed,
        out_specs=(
            P("snap", "space"),
            P(None, "space", "snap", None),
            P(None, "space", "snap", None),
        ),
        check_vma=False,
    )
```

```python
import functools
import math

import jax
import jax.numpy as jnp
from jax import lax
from jax.experimental import pallas as pl
from jax.experimental.pallas import tpu as pltpu
from jax.sharding import PartitionSpec as P

GROUP = 4
HALO = 2
STEP = 32
SWEEP_COST = 10000
CHUNKS = (1, 1)
EXTRA = 4
VMEM = 14 * 1024 * 1024

SLOW = pl.BlockSpec(memory_space=pltpu.HBM)
FAST = pl.BlockSpec(memory_space=pltpu.VMEM)
SCALAR = pl.BlockSpec(memory_space=pltpu.SMEM)


def call(kernel, name, in_specs, out_shape, scratch, flops, *operands):
    return pl.pallas_call(
        kernel,
        in_specs=in_specs,
        out_specs=jax.tree.map(lambda _: FAST, out_shape),
        out_shape=out_shape,
        scratch_shapes=scratch,
        compiler_params=pltpu.CompilerParams(vmem_limit_bytes=VMEM),
        cost_estimate=pl.CostEstimate(flops=flops, bytes_accessed=1024, transcendentals=0),
        name=name,
    )(*operands)


def pack_kernel(plan, info, source, conductance, token, *refs):
    outs, field, sems = refs[:-2], refs[-2], refs[-1]
    member, core = info[0], info[1]
    copies, more = [], []
    values = conductance[0]
    high = values.astype(jnp.bfloat16)
    rest = values - high.astype(jnp.float32)
    middle = rest.astype(jnp.bfloat16)

    def add(group, source, target):
        copy = pltpu.make_async_copy(source, target, sems.at[len(copies) + len(more)])
        group.append(copy)

    for out, pieces in zip(outs, plan):
        at = 0
        for kind, *what in pieces:
            if kind == "set":
                blocks, _, block = source.shape[:3]
                for i in range(blocks):
                    add(copies, source.at[i, member ^ what[0]], out.at[pl.ds(at + i * block, block)])
                at += blocks * block
                add(more, field, out.at[pl.ds(at, EXTRA)])
                at += EXTRA
            else:
                start, size, flip = what
                spot = start + (1 - core if flip else core) * size
                add(copies, source.at[pl.ds(spot, size)], out.at[pl.ds(at, size)])
                at += size
    for copy in copies:
        copy.start()
    field[0] = high
    field[1] = middle
    field[2] = (rest - middle.astype(jnp.float32)).astype(jnp.bfloat16)
    field[3] = jnp.zeros_like(high)
    for copy in more:
        copy.start()
    for copy in copies + more:
        copy.wait()


def pack(info, source, conductance, token, plan):
    blocks, block = source.shape[0], source.shape[2]
    width_y, width_z = source.shape[-2:]
    lengths = {"set": lambda what: blocks * block + EXTRA, "half": lambda what: what[1]}
    shapes, count = [], 0
    for pieces in plan:
        entries = sum(lengths[kind](what) for kind, *what in pieces)
        shapes.append(jax.ShapeDtypeStruct((entries, width_y, width_z), source.dtype))
        count += sum(blocks + 1 if piece[0] == "set" else 1 for piece in pieces)
    scratch = [pltpu.VMEM((EXTRA, width_y, width_z), source.dtype), pltpu.SemaphoreType.DMA((count,))]
    return call(
        functools.partial(pack_kernel, plan),
        "pack",
        [SCALAR, SLOW, FAST, pl.BlockSpec(memory_space=pl.ANY)],
        shapes,
        scratch,
        1000,
        info,
        source,
        conductance,
        token,
    )


def join_kernel(*refs):
    out, at = refs[-1], 0
    for ref in refs[:-1]:
        out[at : at + ref.shape[0]] = ref[...]
        at += ref.shape[0]


def join(*arrays):
    shape = (sum(a.shape[0] for a in arrays),) + arrays[0].shape[1:]
    out_shape = jax.ShapeDtypeStruct(shape, arrays[0].dtype)
    return call(join_kernel, "join", [FAST] * len(arrays), out_shape, [], 1000, *arrays)


def along_z(rows, band):
    high = rows.astype(jnp.bfloat16)
    low = (rows - high.astype(jnp.float32)).astype(jnp.bfloat16)
    both = jnp.concatenate([high, low], axis=1)
    return jnp.dot(both, band[...], preferred_element_type=jnp.float32)


def sweep_kernel(adjoint, layout, begin, lead, place, *refs):
    planes = GROUP + 2 * HALO
    arrays = 1 + max(number for number, _ in layout)
    sources = [(refs[number], offset) for number, offset in layout]
    shift, band = refs[arrays], refs[arrays + 1]
    if lead is None:
        cond, out = refs[arrays + 2], refs[arrays + 3]
    else:
        out, cond = refs[arrays + 2], refs[arrays + 3]
    inverse, flat, start, gain, first, lateral = refs[-6:]
    _, width_y, step, width_z = start.shape
    count = out.shape[0]

    if adjoint:
        inverse[...] = 1.0 / cond[HALO : planes - HALO]
    if lead is not None:
        for slot, (source, offset) in enumerate(sources):
            terms = [source[offset + lead + i].astype(jnp.float32) for i in range(3)]
            cond[place[slot]] = (terms[0] + terms[1]) + terms[2]

    def relax(old, low, high, put):
        for plane in range(low, high):
            rows = old[plane].reshape(width_y * step, width_z)
            lateral[...] = along_z(rows, band).reshape(width_y, step, width_z)
            for y in range(width_y):
                total = old[plane - 1, y] + old[plane + 1, y]
                if y > 0:
                    total = total + old[plane, y - 1]
                if y < width_y - 1:
                    total = total + old[plane, y + 1]
                put(plane, y, start[plane, y] + gain[plane, y] * (total + lateral[y]))

    def keep(plane, y, state):
        first[plane, y] = state

    def one_pass(number, carry):
        at = pl.multiple_of(number * step, step)
        level = shift[pl.ds(begin + at, step), :]
        for slot, (source, offset) in enumerate(sources):
            plane = place[slot]
            piece = source[pl.ds(offset + begin + at, step)].astype(jnp.float32)
            flat[slot] = piece.reshape(step * width_y, width_z)
            for y in range(width_y):
                coeff = cond[plane, pl.ds(y, 1), :]
                diag = level + 6.0 * coeff
                guess = pltpu.reciprocal(diag, approx=True)
                recip = guess * (2.0 - diag * guess)
                scaled = recip * coeff
                force = flat[slot, pl.ds(y, step, stride=width_y), :]
                gain[plane, y] = scaled
                start[plane, y] = force * (scaled if adjoint else recip)

        def emit(plane, y, state):
            if adjoint:
                state = state * inverse[plane - HALO, pl.ds(y, 1), :]
            spot = ((plane - HALO) * width_y + y) * width_z
            out[pl.ds(at, step), spot : spot + width_z] = state.astype(jnp.bfloat16)

        relax(start, 1, planes - 1, keep)
        relax(first, HALO, planes - HALO, emit)
        return carry

    lax.fori_loop(0, count // step, one_pass, 0)


def sweep(adjoint, place, pair, near, far, early, late_near, late_far, shift, band, cond, span=None):
    width_z = shift.shape[1]
    begin, count = span or (0, shift.shape[0])
    sources = [pair, near, far, early, late_near, late_far]
    size = near.shape[0]
    layout = [(0, 0), (0, size), (1, 0), (2, 0), (3, 0), (3, size), (4, 0), (5, 0)]
    width_y = near.shape[1]
    planes = GROUP + 2 * HALO
    step = min(STEP, count)
    cells = GROUP * width_y * width_z
    out_shape = [jax.ShapeDtypeStruct((count, cells), jnp.bfloat16)]
    if cond is None:
        out_shape += [jax.ShapeDtypeStruct((planes, width_y, width_z), jnp.float32)]
    field = pltpu.VMEM((planes, width_y, step, width_z), jnp.float32)
    scratch = [
        pltpu.VMEM((GROUP, width_y, width_z), jnp.float32),
        pltpu.VMEM((planes, step * width_y, width_z), jnp.float32),
        field,
        field,
        field,
        pltpu.VMEM((width_y, step, width_z), jnp.float32),
    ]
    operands = [place, *sources, shift, band] + ([] if cond is None else [cond])
    return call(
        functools.partial(sweep_kernel, adjoint, layout, begin, shift.shape[0] if cond is None else None),
        "adjoint_sweeps" if adjoint else "direct_sweeps",
        [SCALAR] + [FAST] * (len(operands) - 1),
        out_shape,
        scratch,
        SWEEP_COST * count * cells,
        *operands,
    )


def scaled_factors(factors, singular):
    return (factors * (1.0 / jnp.sqrt(singular[...]))).astype(jnp.bfloat16)


def slab(refs, at, depth):
    span = pl.ds(pl.multiple_of(at, 128), depth)
    return jnp.concatenate([ref[:, span] for ref in refs], axis=0)


def gram_kernel(start, blocks, parts, splits, last, info, factors, singular, *refs):
    own, far, direct = refs[:splits], refs[splits : 2 * splits], refs[2 * splits : 2 * splits + parts]
    rest = refs[2 * splits + parts :]
    if last:
        older, older_modes = rest[:2]
        rest = rest[2:]
        kept, sent, kept_modes, sent_modes = rest[0], rest[1:-4], rest[-4], rest[-3]
        pieces, modes = rest[-2:]
    else:
        pieces, modes = rest
    member, core, share = info[0], info[1], info[2]
    half, cells = splits * own[0].shape[0], own[0].shape[1]
    count, _, width = pieces.shape
    depth = cells // GROUP
    dims = (((1,), (1,)), ((), ()))
    total = jnp.zeros((2 * half, count * width), jnp.float32)
    for plane in range(GROUP):
        rows, cols = slab((*own, *far), plane * depth, depth), slab(direct, plane * depth, depth)
        total = total + lax.dot_general(rows, cols, dims, preferred_element_type=jnp.float32)
    for side in range(2):
        first = jnp.where(side == 0, core, 1 - core) * half
        spot = pl.ds(pl.multiple_of(first, half), half)
        for part in range(count):
            pieces[part, spot, :] = total[side * half : (side + 1) * half, part * width : (part + 1) * width]
    left = scaled_factors(factors[:, start : start + 2 * half], singular)
    lower, upper = left[:, :half], left[:, half:]
    swapped = jnp.concatenate(
        [jnp.where(core == 0, lower, upper), jnp.where(core == 0, upper, lower)], axis=1
    )
    term = jnp.dot(swapped, slab((*own, *far), member * depth, depth), preferred_element_type=jnp.float32)
    if not last:
        modes[...] = term
        return
    modes[...] = older_modes[...] + term
    for number in range(len(sent) + 1):
        index = info[4 + number]
        if number == 0:
            kept[0:start, :] = older[index]
            kept[start:, :] = pieces[index]
        else:
            sent[number - 1][0:start, :] = older[index].astype(jnp.bfloat16)
            sent[number - 1][start:, :] = pieces[index].astype(jnp.bfloat16)
    shares = sent_modes.shape[0] + 1
    wide = depth // shares
    for step in range(shares):
        piece = modes[:, pl.ds(pl.multiple_of(((share + step) % shares) * wide, wide), wide)]
        if step == 0:
            kept_modes[...] = piece
        else:
            sent_modes[step - 1] = piece.astype(jnp.bfloat16)


def gram_part(info, start, own, far, factors, singular, direct, blocks, older, layers):
    half, cells = len(own) * own[0].shape[0], own[0].shape[1]
    width = direct[0].shape[0]
    mode_count, rows = factors.shape
    shares = len(direct) // blocks
    depth = cells // GROUP
    pieces = (shares * blocks, 2 * half, width)
    operands = [info, factors, singular, *own, *far, *direct]
    if older is None:
        out_shape = [
            jax.ShapeDtypeStruct(pieces, jnp.float32),
            jax.ShapeDtypeStruct((mode_count, depth), jnp.float32),
        ]
        scratch = []
    else:
        operands += older
        out_shape = [jax.ShapeDtypeStruct((rows, width), jnp.float32)]
        out_shape += [jax.ShapeDtypeStruct((rows, width), jnp.bfloat16)] * (layers - 1)
        out_shape += [
            jax.ShapeDtypeStruct((mode_count, depth // shares), jnp.float32),
            jax.ShapeDtypeStruct((shares - 1, mode_count, depth // shares), jnp.bfloat16),
        ]
        scratch = [pltpu.VMEM(pieces, jnp.float32), pltpu.VMEM((mode_count, depth), jnp.float32)]
    return call(
        functools.partial(gram_kernel, start, blocks, len(direct), len(own), older is not None),
        "gram_part",
        [SCALAR] + [FAST] * (len(operands) - 1),
        out_shape,
        scratch,
        2 * half * cells,
        *operands,
    )


def modes_kernel(parts, shares, info, factors, singular, *refs):
    direct, kept, sent = refs[:parts], refs[parts], refs[parts + 1 :]
    member, share = info[0], info[2]
    depth = direct[0].shape[1] // GROUP
    wide = depth // shares
    right = scaled_factors(factors[...], singular)
    for mask in range(GROUP):
        at = (member ^ mask) * depth + share * wide
        term = jnp.dot(right, slab(direct, at, wide), preferred_element_type=jnp.float32)
        if mask == 0:
            kept[...] = term
        else:
            sent[mask - 1][...] = term.astype(jnp.bfloat16)


def direct_part(info, factors, singular, direct, shares):
    width, cells = direct[0].shape
    shape = (factors.shape[0], cells // GROUP // shares)
    operands = [info, factors, singular, *direct]
    return call(
        functools.partial(modes_kernel, len(direct), shares),
        "direct_modes_part",
        [SCALAR] + [FAST] * (len(operands) - 1),
        [jax.ShapeDtypeStruct(shape, jnp.float32)] + [jax.ShapeDtypeStruct(shape, jnp.bfloat16)] * (GROUP - 1),
        [],
        width * cells,
        *operands,
    )


def band_matrix(width):
    near = (jnp.abs(jnp.arange(width)[:, None] - jnp.arange(width)[None, :]) == 1).astype(jnp.bfloat16)
    return jnp.concatenate([near, near])


def lookup(indices, shift_list):
    levels = jnp.arange(shift_list.shape[0], dtype=jnp.int32)
    picked = jnp.where(indices[:, None] == levels[None, :], shift_list[None, :], jnp.float32(0.0))
    return jnp.sum(picked, axis=1)


def pick(array, index, axis=0):
    return lax.dynamic_index_in_dim(array, index, axis, keepdims=False)


def after(array, *others):
    return lax.optimization_barrier((array, *others))[0]


def per_device(
    forcing_direct,
    forcing_adjoint,
    conductance,
    shift_table,
    freq_direct,
    freq_adjoint,
    left_factors,
    right_factors,
    singular_values,
):
    n_space, n_snap = lax.axis_size("space"), lax.axis_size("snap")
    rows, plane_x, width_y, width_z = forcing_direct.shape
    layers = n_space // GROUP
    block = rows * n_snap // n_space
    blocks = rows // (GROUP * block)
    mode_count = left_factors.shape[1]
    rows_y = width_y // n_snap
    weight = 1.0 / math.sqrt(plane_x * n_space * width_y * width_z)

    spot, share = lax.axis_index("space"), lax.axis_index("snap")
    layer, member = spot // GROUP, spot % GROUP
    core, high = member % 2, member // 2

    def piece_index(target):
        return ((share - target // blocks) % n_snap) * blocks + target % blocks

    info = jnp.stack(
        [member, core, share, layer] + [piece_index((layer + step) % layers) for step in range(layers)]
    ).astype(jnp.int32)

    def swap(array, mask):
        return lax.ppermute(array, "space", [(i, i ^ mask) for i in range(n_space)])

    def around(array, step):
        return lax.ppermute(array, "snap", [(i, (i + step) % n_snap) for i in range(n_snap)])

    ups = [(i, i + GROUP) for i in range(n_space - GROUP)]
    downs = [(i + GROUP, i) for i in range(n_space - GROUP)]
    upper = lambda pairs, wanted: [p for p in pairs if (p[0] % GROUP) // 2 == wanted]
    early = lambda array: lax.ppermute(array, "space", upper(ups, 1) + upper(downs, 0))
    late = lambda array: lax.ppermute(array, "space", upper(ups, 0) + upper(downs, 1))

    sizes = [rows * part // sum(CHUNKS) // 2 for part in CHUNKS]
    starts = [2 * sum(sizes[:i]) for i in range(len(sizes))]
    sets = forcing_direct.reshape(blocks, GROUP, block, width_y, width_z)
    rows_adj = forcing_adjoint.reshape(rows, width_y, width_z)
    own = lambda i: ("half", starts[i], sizes[i], False)
    cross = lambda i: ("half", starts[i], sizes[i], True)
    near_d, far_d, cross_d, own_d = pack(info, sets, conductance, info, [[("set", mask)] for mask in (2, 3, 1, 0)])
    crossed_d = swap(cross_d, 1)
    to_core, own_0, cross_0, own_1, cross_1 = pack(
        info, rows_adj, conductance, crossed_d, [[cross(0), cross(1)], [own(0)], [cross(0)], [own(1)], [cross(1)]]
    )

    wide = lambda values: jnp.broadcast_to(values[:, None], (values.shape[0], width_z))
    dir_levels = lookup(freq_direct, shift_table).reshape(blocks, GROUP, block)
    dir_shift = wide(pick(dir_levels, member, 1).reshape(-1))
    adj_levels = lookup(freq_adjoint, shift_table)
    adj_shift = [
        wide(lax.dynamic_slice_in_dim(adj_levels, at + core * size, size, 0)) for at, size in zip(starts, sizes)
    ]
    inside = lambda index: HALO + index
    below = lambda index: index - HALO
    above = lambda index: index + GROUP + HALO
    place = jnp.stack(
        [inside(member ^ k) for k in range(4)]
        + [jnp.where(high == 1, below(member ^ k), above(member ^ k)) for k in (0, 1)]
        + [jnp.where(high == 1, above(member ^ k), below(member ^ k)) for k in (2, 3)]
    ).astype(jnp.int32)
    band = band_matrix(width_z)

    y_0, y_1 = swap(near_d, 2), swap(far_d, 3)
    crossed = swap(to_core, 1)
    pair_d = join(own_d, crossed_d)
    pair_0, pair_1 = join(own_0, crossed[: sizes[0]]), join(own_1, crossed[sizes[0] :])
    e_d = early(pair_d)
    l_0, l_1 = late(y_0), late(y_1)
    y_2 = swap(after(own_0, y_1), 2)
    y_3 = swap(after(cross_0, y_0, pair_d, pair_0, pair_1), 3)
    e_0 = early(after(pair_0, y_0))
    dir_state, cond = sweep(False, place, pair_d, y_0, y_1, e_d, l_0, l_1, dir_shift, band, None, (0, block))
    dir_states = [dir_state] + [
        sweep(False, place, pair_d, y_0, y_1, e_d, l_0, l_1, dir_shift, band, cond, (i * block, block))[0]
        for i in range(1, blocks)
    ]
    dir_state = dir_states[-1]
    moved = [[around(state, step) for state in dir_states] for step in range(1, n_snap)]
    everyone = dir_states + [state for states in moved for state in states]
    l_2, l_3 = late(y_2), late(after(y_3, dir_state))
    y_4 = swap(after(own_1, y_2, l_0), 2)
    y_5 = swap(after(cross_1, y_3, dir_state), 3)
    e_1 = early(after(pair_1, y_4))
    l_4 = late(after(y_4, l_2))
    state_0 = sweep(True, place, pair_0, y_2, after(y_3, y_4, everyone[blocks]), e_0, l_2, l_3, adj_shift[0], band, cond)[0]
    other_0 = swap(state_0, 1)
    l_5 = late(after(y_5, state_0, l_4))
    part = sizes[1] // 2
    state_1 = [
        sweep(True, place, pair_1, y_4, after(y_5, everyone[-1]), e_1, l_4, l_5, adj_shift[1], band, cond, (at, part))[0]
        for at in (0, part)
    ]
    other_1 = [swap(state, 1) for state in state_1]

    singular = singular_values.reshape(1, mode_count).T
    left = lax.dynamic_slice_in_dim(left_factors.T, share * rows, rows, 1)
    right_sets = right_factors.T.reshape(mode_count, n_snap, blocks, GROUP, block)
    right_sets = pick(right_sets, member, 3).reshape(mode_count, n_snap, blocks * block)
    right = jnp.concatenate([pick(right_sets, (share - step) % n_snap, 1) for step in range(n_snap)], axis=1)
    kept, *sent = direct_part(info, right, singular, everyone, n_snap)
    for mask in range(1, GROUP):
        kept = kept + swap(sent[mask - 1], mask).astype(jnp.float32)
    direct_modes = kept.reshape(mode_count, 1, rows_y, width_z)

    outs = gram_part(info, 0, [state_0], [other_0], left, singular, everyone, blocks, None, layers)
    outs = gram_part(
        info, starts[1], state_1, other_1, left, singular, everyone, blocks, list(outs), layers
    )
    kept, *sent, kept_modes, sent_modes = outs
    for step in range(1, layers):
        pairs = [(i, (i + GROUP * step) % n_space) for i in range(n_space)]
        kept = kept + lax.ppermute(sent[step - 1], "space", pairs).astype(jnp.float32)
    gram = kept * weight
    for step in range(1, n_snap):
        kept_modes = kept_modes + around(sent_modes[step - 1], step).astype(jnp.float32)
    adjoint_modes = kept_modes.reshape(mode_count, 1, rows_y, width_z)
    return (gram, direct_modes, adjoint_modes)


def solution(mesh):
    placed = (
        P("snap", "space", None, None),
        P("snap", "space", None, None),
        P("space", None, None),
        P(),
        P("snap"),
        P("snap"),
        P(),
        P(),
        P(),
    )
    return jax.shard_map(
        per_device,
        mesh=mesh,
        in_specs=placed,
        out_specs=(
            P("snap", "space"),
            P(None, "space", "snap", None),
            P(None, "space", "snap", None),
        ),
        check_vma=False,
    )
```

```python
import functools
import math

import jax
import jax.numpy as jnp
from jax import lax
from jax.experimental import pallas as pl
from jax.experimental.pallas import tpu as pltpu
from jax.sharding import PartitionSpec as P

GROUP = 4
HALO = 2
STEP = 32
SWEEP_COST = 5000
CHUNKS = (3, 3, 2)
EXTRA = 4
VMEM = 20 * 1024 * 1024

SLOW = pl.BlockSpec(memory_space=pltpu.HBM)
FAST = pl.BlockSpec(memory_space=pltpu.VMEM)
SCALAR = pl.BlockSpec(memory_space=pltpu.SMEM)


def call(kernel, name, in_specs, out_shape, scratch, flops, *operands):
    return pl.pallas_call(
        kernel,
        in_specs=in_specs,
        out_specs=jax.tree.map(lambda _: FAST, out_shape),
        out_shape=out_shape,
        scratch_shapes=scratch,
        compiler_params=pltpu.CompilerParams(vmem_limit_bytes=VMEM),
        cost_estimate=pl.CostEstimate(flops=flops, bytes_accessed=1024, transcendentals=0),
        name=name,
    )(*operands)


def pack_kernel(plan, info, source, conductance, token, *refs):
    outs, field, sems = refs[:-2], refs[-2], refs[-1]
    member, core = info[0], info[1]
    copies, more = [], []
    values = conductance[0]
    high = values.astype(jnp.bfloat16)
    rest = values - high.astype(jnp.float32)
    middle = rest.astype(jnp.bfloat16)

    def add(group, source, target):
        copy = pltpu.make_async_copy(source, target, sems.at[len(copies) + len(more)])
        group.append(copy)

    for out, pieces in zip(outs, plan):
        at = 0
        for kind, *what in pieces:
            if kind == "set":
                blocks, _, block = source.shape[:3]
                for i in range(blocks):
                    add(copies, source.at[i, member ^ what[0]], out.at[pl.ds(at + i * block, block)])
                at += blocks * block
                add(more, field, out.at[pl.ds(at, EXTRA)])
                at += EXTRA
            else:
                start, size, flip = what
                spot = start + (1 - core if flip else core) * size
                add(copies, source.at[pl.ds(spot, size)], out.at[pl.ds(at, size)])
                at += size
    for copy in copies:
        copy.start()
    field[0] = high
    field[1] = middle
    field[2] = (rest - middle.astype(jnp.float32)).astype(jnp.bfloat16)
    field[3] = jnp.zeros_like(high)
    for copy in more:
        copy.start()
    for copy in copies + more:
        copy.wait()


def pack(info, source, conductance, token, plan):
    blocks, block = source.shape[0], source.shape[2]
    width_y, width_z = source.shape[-2:]
    lengths = {"set": lambda what: blocks * block + EXTRA, "half": lambda what: what[1]}
    shapes, count = [], 0
    for pieces in plan:
        entries = sum(lengths[kind](what) for kind, *what in pieces)
        shapes.append(jax.ShapeDtypeStruct((entries, width_y, width_z), source.dtype))
        count += sum(blocks + 1 if piece[0] == "set" else 1 for piece in pieces)
    scratch = [pltpu.VMEM((EXTRA, width_y, width_z), source.dtype), pltpu.SemaphoreType.DMA((count,))]
    return call(
        functools.partial(pack_kernel, plan),
        "pack",
        [SCALAR, SLOW, FAST, pl.BlockSpec(memory_space=pl.ANY)],
        shapes,
        scratch,
        1000,
        info,
        source,
        conductance,
        token,
    )


def join_kernel(start, own, other, out):
    size = own.shape[0]
    out[:size] = own[...]
    out[size:] = other[start : start + size]


def join(own, other, start):
    shape = (2 * own.shape[0],) + own.shape[1:]
    out_shape = jax.ShapeDtypeStruct(shape, own.dtype)
    kernel = functools.partial(join_kernel, start)
    return call(kernel, "join", [FAST] * 2, out_shape, [], 1000, own, other)


def along_z(rows, band):
    high = rows.astype(jnp.bfloat16)
    low = (rows - high.astype(jnp.float32)).astype(jnp.bfloat16)
    both = jnp.concatenate([high, low], axis=1)
    return jnp.dot(both, band[...], preferred_element_type=jnp.float32)


def sweep_kernel(adjoint, layout, begin, lead, place, *refs):
    planes = GROUP + 2 * HALO
    arrays = 1 + max(number for number, _ in layout)
    sources = [(refs[number], offset) for number, offset in layout]
    shift, band = refs[arrays], refs[arrays + 1]
    if lead is None:
        cond, out = refs[arrays + 2], refs[arrays + 3]
    else:
        out, cond = refs[arrays + 2], refs[arrays + 3]
    inverse, flat, start, gain, first, lateral = refs[-6:]
    _, width_y, step, width_z = start.shape
    count = out.shape[0]

    if adjoint:
        inverse[...] = 1.0 / cond[HALO : planes - HALO]
    if lead is not None:
        for slot, (source, offset) in enumerate(sources):
            terms = [source[offset + lead + i].astype(jnp.float32) for i in range(3)]
            cond[place[slot]] = (terms[0] + terms[1]) + terms[2]

    def relax(old, low, high, put):
        for plane in range(low, high):
            rows = old[plane].reshape(width_y * step, width_z)
            lateral[...] = along_z(rows, band).reshape(width_y, step, width_z)
            for y in range(width_y):
                total = old[plane - 1, y] + old[plane + 1, y]
                if y > 0:
                    total = total + old[plane, y - 1]
                if y < width_y - 1:
                    total = total + old[plane, y + 1]
                put(plane, y, start[plane, y] + gain[plane, y] * (total + lateral[y]))

    def keep(plane, y, state):
        first[plane, y] = state

    def one_pass(number, carry):
        at = pl.multiple_of(number * step, step)
        level = shift[pl.ds(begin + at, step), :]
        for slot, (source, offset) in enumerate(sources):
            plane = place[slot]
            piece = source[pl.ds(offset + begin + at, step)].astype(jnp.float32)
            flat[slot] = piece.reshape(step * width_y, width_z)
            for y in range(width_y):
                coeff = cond[plane, pl.ds(y, 1), :]
                diag = level + 6.0 * coeff
                guess = pltpu.reciprocal(diag, approx=True)
                recip = guess * (2.0 - diag * guess)
                scaled = recip * coeff
                force = flat[slot, pl.ds(y, step, stride=width_y), :]
                gain[plane, y] = scaled
                start[plane, y] = force * (scaled if adjoint else recip)

        def emit(plane, y, state):
            if adjoint:
                state = state * inverse[plane - HALO, pl.ds(y, 1), :]
            spot = ((plane - HALO) * width_y + y) * width_z
            out[pl.ds(at, step), spot : spot + width_z] = state.astype(jnp.bfloat16)

        relax(start, 1, planes - 1, keep)
        relax(first, HALO, planes - HALO, emit)
        return carry

    lax.fori_loop(0, count // step, one_pass, 0)


def sweep(adjoint, place, sources, shift, band, cond, span=None):
    width_z = shift.shape[1]
    begin, count = span or (0, shift.shape[0])
    size = sources[0].shape[0] // 2
    layout = [(i, at) for i, array in enumerate(sources) for at in range(0, array.shape[0], size)]
    width_y = sources[0].shape[1]
    planes = GROUP + 2 * HALO
    step = STEP if count % STEP == 0 else STEP // 2
    cells = GROUP * width_y * width_z
    out_shape = [jax.ShapeDtypeStruct((count, cells), jnp.bfloat16)]
    if cond is None:
        out_shape += [jax.ShapeDtypeStruct((planes, width_y, width_z), jnp.float32)]
    field = pltpu.VMEM((planes, width_y, step, width_z), jnp.float32)
    scratch = [
        pltpu.VMEM((GROUP, width_y, width_z), jnp.float32),
        pltpu.VMEM((planes, step * width_y, width_z), jnp.float32),
        field,
        field,
        field,
        pltpu.VMEM((width_y, step, width_z), jnp.float32),
    ]
    operands = [place, *sources, shift, band] + ([] if cond is None else [cond])
    return call(
        functools.partial(sweep_kernel, adjoint, layout, begin, shift.shape[0] if cond is None else None),
        "adjoint_sweeps" if adjoint else "direct_sweeps",
        [SCALAR] + [FAST] * (len(operands) - 1),
        out_shape,
        scratch,
        SWEEP_COST * count * cells,
        *operands,
    )


def scaled_factors(factors, singular):
    return (factors * (1.0 / jnp.sqrt(singular[...]))).astype(jnp.bfloat16)


def slab(refs, at, depth):
    span = pl.ds(pl.multiple_of(at, 128), depth)
    return jnp.concatenate([ref[:, span] for ref in refs], axis=0)


def gram_kernel(start, chunks, parts, shares, last, info, factors, singular, *refs):
    own, far, direct = refs[:chunks], refs[chunks : 2 * chunks], refs[2 * chunks : 2 * chunks + parts]
    rest = refs[2 * chunks + parts :]
    if last:
        older, older_modes = rest[:2]
        rest = rest[2:]
        kept, sent, kept_modes, sent_modes = rest[0], rest[1:-4], rest[-4], rest[-3]
    pieces, modes = rest[-2:]
    member, core, share = info[0], info[1], info[2]
    adjoint = [ref for pair in zip(own, far) for ref in pair]
    rows_total, cells = sum(ref.shape[0] for ref in adjoint), own[0].shape[1]
    count, _, width = pieces.shape
    depth = cells // GROUP
    dims = (((1,), (1,)), ((), ()))
    total = jnp.zeros((rows_total, count * width), jnp.float32)
    for plane in range(GROUP):
        rows, cols = slab(adjoint, plane * depth, depth), slab(direct, plane * depth, depth)
        total = total + lax.dot_general(rows, cols, dims, preferred_element_type=jnp.float32)
    per_share = factors.shape[1] // shares
    window = factors[:, pl.ds(pl.multiple_of(share * per_share, per_share), per_share)]
    window = scaled_factors(window[:, start : start + rows_total], singular)
    left, at = [], 0
    for ref in own:
        half = ref.shape[0]
        for side in range(2):
            spot = pl.ds(pl.multiple_of(at + jnp.where(side == 0, core, 1 - core) * half, 16), half)
            held = at + side * half
            for part in range(count):
                pieces[part, spot, :] = total[held : held + half, part * width : (part + 1) * width]
        lower, upper = window[:, at : at + half], window[:, at + half : at + 2 * half]
        left += [jnp.where(core == 0, lower, upper), jnp.where(core == 0, upper, lower)]
        at += 2 * half
    term = jnp.dot(
        jnp.concatenate(left, axis=1), slab(adjoint, member * depth, depth), preferred_element_type=jnp.float32
    )
    if not last:
        modes[...] = term
        return
    modes[...] = older_modes[...] + term
    for number in range(len(sent) + 1):
        index = info[4 + number]
        if number == 0:
            kept[0:start, :] = older[index]
            kept[start:, :] = pieces[index]
        else:
            sent[number - 1][0:start, :] = older[index].astype(jnp.bfloat16)
            sent[number - 1][start:, :] = pieces[index].astype(jnp.bfloat16)
    wide = depth // shares
    for step in range(shares):
        piece = modes[:, pl.ds(pl.multiple_of(((share + step) % shares) * wide, wide), wide)]
        if step == 0:
            kept_modes[...] = piece
        else:
            sent_modes[step - 1] = piece.astype(jnp.bfloat16)


def gram_part(info, start, own, far, factors, singular, direct, blocks, older, layers):
    cells = own[0].shape[1]
    width = direct[0].shape[0]
    shares = len(direct) // blocks
    mode_count, rows = factors.shape[0], factors.shape[1] // shares
    depth = cells // GROUP
    height = 2 * sum(a.shape[0] for a in own)
    pieces = (shares * blocks, height, width)
    operands = [info, factors, singular, *own, *far, *direct]
    if older is None:
        out_shape = [
            jax.ShapeDtypeStruct(pieces, jnp.float32),
            jax.ShapeDtypeStruct((mode_count, depth), jnp.float32),
        ]
        scratch = []
    else:
        operands += older
        out_shape = [jax.ShapeDtypeStruct((rows, width), jnp.float32)]
        out_shape += [jax.ShapeDtypeStruct((rows, width), jnp.bfloat16)] * (layers - 1)
        out_shape += [
            jax.ShapeDtypeStruct((mode_count, depth // shares), jnp.float32),
            jax.ShapeDtypeStruct((shares - 1, mode_count, depth // shares), jnp.bfloat16),
        ]
        scratch = [pltpu.VMEM(pieces, jnp.float32), pltpu.VMEM((mode_count, depth), jnp.float32)]
    return call(
        functools.partial(gram_kernel, start, len(own), len(direct), shares, older is not None),
        "gram_part",
        [SCALAR] + [FAST] * (len(operands) - 1),
        out_shape,
        scratch,
        height * cells,
        *operands,
    )


def modes_kernel(parts, shares, info, factors, singular, *refs):
    direct, kept, sent = refs[:parts], refs[parts], refs[parts + 1 :]
    member, share = info[0], info[2]
    depth = direct[0].shape[1] // GROUP
    wide = depth // shares
    width = direct[0].shape[0]
    blocks = parts // shares

    def columns(owner, number):
        base = (owner * blocks + number) * GROUP * width
        spans = [factors[:, base + i * width : base + (i + 1) * width] for i in range(GROUP)]
        return sum(jnp.where(member == i, span, 0.0) for i, span in enumerate(spans))

    right = []
    for part in range(parts):
        owner = (share + shares - part // blocks) % shares
        right.append(sum(jnp.where(owner == i, columns(i, part % blocks), 0.0) for i in range(shares)))
    right = scaled_factors(jnp.concatenate(right, axis=1), singular)
    for mask in range(GROUP):
        at = (member ^ mask) * depth + share * wide
        term = jnp.dot(right, slab(direct, at, wide), preferred_element_type=jnp.float32)
        if mask == 0:
            kept[...] = term
        else:
            sent[mask - 1][...] = term.astype(jnp.bfloat16)


def direct_part(info, factors, singular, direct, shares):
    width, cells = direct[0].shape
    shape = (factors.shape[0], cells // GROUP // shares)
    operands = [info, factors, singular, *direct]
    return call(
        functools.partial(modes_kernel, len(direct), shares),
        "direct_modes_part",
        [SCALAR] + [FAST] * (len(operands) - 1),
        [jax.ShapeDtypeStruct(shape, jnp.float32)] + [jax.ShapeDtypeStruct(shape, jnp.bfloat16)] * (GROUP - 1),
        [],
        width * cells,
        *operands,
    )


def band_matrix(width):
    near = (jnp.abs(jnp.arange(width)[:, None] - jnp.arange(width)[None, :]) == 1).astype(jnp.bfloat16)
    return jnp.concatenate([near, near])


def lookup(indices, shift_list):
    levels = jnp.arange(shift_list.shape[0], dtype=jnp.int32)
    picked = jnp.where(indices[:, None] == levels[None, :], shift_list[None, :], jnp.float32(0.0))
    return jnp.sum(picked, axis=1)


def pick(array, index, axis=0):
    return lax.dynamic_index_in_dim(array, index, axis, keepdims=False)


def after(array, *others):
    return lax.optimization_barrier((array, *others))[0]


def per_device(
    forcing_direct,
    forcing_adjoint,
    conductance,
    shift_table,
    freq_direct,
    freq_adjoint,
    left_factors,
    right_factors,
    singular_values,
):
    n_space, n_snap = lax.axis_size("space"), lax.axis_size("snap")
    rows, plane_x, width_y, width_z = forcing_direct.shape
    layers = n_space // GROUP
    block = rows * n_snap // n_space
    blocks = rows // (GROUP * block)
    mode_count = left_factors.shape[1]
    rows_y = width_y // n_snap
    weight = 1.0 / math.sqrt(plane_x * n_space * width_y * width_z)

    spot, share = lax.axis_index("space"), lax.axis_index("snap")
    layer, member = spot // GROUP, spot % GROUP
    core, high = member % 2, member // 2

    def piece_index(target):
        return ((share - target // blocks) % n_snap) * blocks + target % blocks

    info = jnp.stack(
        [member, core, share, layer] + [piece_index((layer + step) % layers) for step in range(layers)]
    ).astype(jnp.int32)

    def swap(array, mask):
        return lax.ppermute(array, "space", [(i, i ^ mask) for i in range(n_space)])

    def around(array, step):
        return lax.ppermute(array, "snap", [(i, (i + step) % n_snap) for i in range(n_snap)])

    ups = [(i, i + GROUP) for i in range(n_space - GROUP)]
    downs = [(i + GROUP, i) for i in range(n_space - GROUP)]
    upper = lambda pairs, wanted: [p for p in pairs if (p[0] % GROUP) // 2 == wanted]
    early = lambda array: lax.ppermute(array, "space", upper(ups, 1) + upper(downs, 0))
    late = lambda array: lax.ppermute(array, "space", upper(ups, 0) + upper(downs, 1))

    sizes = [rows * part // sum(CHUNKS) // 32 * 16 for part in CHUNKS[1:]]
    sizes = [rows // 2 - sum(sizes)] + sizes
    starts = [2 * sum(sizes[:i]) for i in range(len(sizes))]
    sets = forcing_direct.reshape(blocks, GROUP, block, width_y, width_z)
    rows_adj = forcing_adjoint.reshape(rows, width_y, width_z)
    own = lambda i: ("half", starts[i], sizes[i], False)
    cross = lambda i: ("half", starts[i], sizes[i], True)
    near_d, far_d, cross_d, own_d = pack(info, sets, conductance, info, [[("set", mask)] for mask in (2, 3, 1, 0)])
    crossed_d = swap(cross_d, 1)
    to_core, *own_adj = pack(
        info,
        rows_adj,
        conductance,
        crossed_d,
        [[cross(i) for i in range(len(sizes))]] + [[own(i)] for i in range(len(sizes))],
    )

    wide = lambda values: jnp.broadcast_to(values[:, None], (values.shape[0], width_z))
    dir_levels = lookup(freq_direct, shift_table).reshape(blocks, GROUP, block)
    dir_shift = wide(pick(dir_levels, member, 1).reshape(-1))
    adj_levels = lookup(freq_adjoint, shift_table)
    adj_shift = [
        wide(lax.dynamic_slice_in_dim(adj_levels, at + core * size, size, 0)) for at, size in zip(starts, sizes)
    ]
    inside = lambda index: HALO + index
    below = lambda index: index - HALO
    above = lambda index: index + GROUP + HALO
    place = jnp.stack(
        [inside(member ^ k) for k in range(4)]
        + [jnp.where(high == 1, below(member ^ k), above(member ^ k)) for k in (0, 1)]
        + [jnp.where(high == 1, above(member ^ k), below(member ^ k)) for k in (2, 3)]
    ).astype(jnp.int32)
    band = band_matrix(width_z)

    near, far = swap(near_d, 2), swap(far_d, 3)
    crossed = swap(to_core, 1)
    pair_d = join(own_d, crossed_d, 0)
    spots = [sum(sizes[:i]) for i in range(len(sizes))]
    pairs = [join(own, crossed, at) for own, at in zip(own_adj, spots)]
    e_d = early(pair_d)
    late_near, late_far = late(near), late(far)
    sources = [pair_d, near, far, e_d, late_near, late_far]
    dir_state, cond = sweep(False, place, sources, dir_shift, band, None, (0, block))
    dir_states = [dir_state] + [
        sweep(False, place, sources, dir_shift, band, cond, (i * block, block))[0] for i in range(1, blocks)
    ]
    moved = [[around(state, step) for state in dir_states] for step in range(1, n_snap)]
    everyone = dir_states + [state for states in moved for state in states]
    y_adj, e_adj, l_adj, own_states, far_states = [], [], [], [], []
    for i, pair in enumerate(pairs):
        y_after = [near, far, late_near] if i == 0 else [y_adj[-1], dir_states[0]]
        e_after = [e_d] if i == 0 else [e_adj[-1], dir_states[-1]]
        y_adj.append(swap(after(pair, *y_after), 2))
        e_adj.append(early(after(pair, *e_after)))
        l_adj.append(late(after(y_adj[i], l_adj[-1]) if i else y_adj[i]))
        arrived = after(y_adj[i], everyone[blocks]) if i == 1 else y_adj[i]
        if i == 2:
            arrived = after(y_adj[i], everyone[-1])
        sources = [pair, arrived, e_adj[i], l_adj[i]]
        own_states.append(sweep(True, place, sources, adj_shift[i], band, cond)[0])
        far_states.append(swap(own_states[i], 1))

    singular = singular_values.reshape(1, mode_count).T
    left, right = left_factors.T, right_factors.T
    kept, *sent = direct_part(info, right, singular, everyone, n_snap)
    for mask in range(1, GROUP):
        kept = kept + swap(sent[mask - 1], mask).astype(jnp.float32)
    direct_modes = kept.reshape(mode_count, 1, rows_y, width_z)

    outs = gram_part(
        info, 0, own_states[:-1], far_states[:-1], left, singular, everyone, blocks, None, layers
    )
    outs = gram_part(
        info, starts[-1], own_states[-1:], far_states[-1:], left, singular, everyone, blocks, list(outs), layers
    )
    kept, *sent, kept_modes, sent_modes = outs
    for step in range(1, layers):
        pairs = [(i, (i + GROUP * step) % n_space) for i in range(n_space)]
        kept = kept + lax.ppermute(sent[step - 1], "space", pairs).astype(jnp.float32)
    gram = kept * weight
    for step in range(1, n_snap):
        kept_modes = kept_modes + around(sent_modes[step - 1], step).astype(jnp.float32)
    adjoint_modes = kept_modes.reshape(mode_count, 1, rows_y, width_z)
    return (gram, direct_modes, adjoint_modes)


def solution(mesh):
    placed = (
        P("snap", "space", None, None),
        P("snap", "space", None, None),
        P("space", None, None),
        P(),
        P("snap"),
        P("snap"),
        P(),
        P(),
        P(),
    )
    return jax.shard_map(
        per_device,
        mesh=mesh,
        in_specs=placed,
        out_specs=(
            P("snap", "space"),
            P(None, "space", "snap", None),
            P(None, "space", "snap", None),
        ),
        check_vma=False,
    )
```

```python
import functools
import math

import jax
import jax.numpy as jnp
from jax import lax
from jax.experimental import pallas as pl
from jax.experimental.pallas import tpu as pltpu
from jax.sharding import PartitionSpec as P

GROUP = 4
HALO = 2
STEP = 32
SWEEP_COST = 6500
CHUNKS = (3, 3, 2)
EXTRA = 4
VMEM = 20 * 1024 * 1024

SLOW = pl.BlockSpec(memory_space=pltpu.HBM)
FAST = pl.BlockSpec(memory_space=pltpu.VMEM)
SCALAR = pl.BlockSpec(memory_space=pltpu.SMEM)


def call(kernel, name, in_specs, out_shape, scratch, flops, *operands):
    return pl.pallas_call(
        kernel,
        in_specs=in_specs,
        out_specs=jax.tree.map(lambda _: FAST, out_shape),
        out_shape=out_shape,
        scratch_shapes=scratch,
        compiler_params=pltpu.CompilerParams(vmem_limit_bytes=VMEM),
        cost_estimate=pl.CostEstimate(flops=flops, bytes_accessed=1024, transcendentals=0),
        name=name,
    )(*operands)


def pack_kernel(plan, info, source, conductance, token, *refs):
    outs, field, sems = refs[:-2], refs[-2], refs[-1]
    member, core = info[0], info[1]
    copies, more = [], []
    values = conductance[0]
    high = values.astype(jnp.bfloat16)
    rest = values - high.astype(jnp.float32)
    middle = rest.astype(jnp.bfloat16)

    def add(group, source, target):
        copy = pltpu.make_async_copy(source, target, sems.at[len(copies) + len(more)])
        group.append(copy)

    for out, pieces in zip(outs, plan):
        at = 0
        for kind, *what in pieces:
            if kind == "set":
                blocks, _, block = source.shape[:3]
                for i in range(blocks):
                    add(copies, source.at[i, member ^ what[0]], out.at[pl.ds(at + i * block, block)])
                at += blocks * block
                add(more, field, out.at[pl.ds(at, EXTRA)])
                at += EXTRA
            else:
                start, size, flip = what
                spot = start + (1 - core if flip else core) * size
                add(copies, source.at[pl.ds(spot, size)], out.at[pl.ds(at, size)])
                at += size
    for copy in copies:
        copy.start()
    field[0] = high
    field[1] = middle
    field[2] = (rest - middle.astype(jnp.float32)).astype(jnp.bfloat16)
    field[3] = jnp.zeros_like(high)
    for copy in more:
        copy.start()
    for copy in copies + more:
        copy.wait()


def pack(info, source, conductance, token, plan):
    blocks, block = source.shape[0], source.shape[2]
    width_y, width_z = source.shape[-2:]
    lengths = {"set": lambda what: blocks * block + EXTRA, "half": lambda what: what[1]}
    shapes, count = [], 0
    for pieces in plan:
        entries = sum(lengths[kind](what) for kind, *what in pieces)
        shapes.append(jax.ShapeDtypeStruct((entries, width_y, width_z), source.dtype))
        count += sum(blocks + 1 if piece[0] == "set" else 1 for piece in pieces)
    scratch = [pltpu.VMEM((EXTRA, width_y, width_z), source.dtype), pltpu.SemaphoreType.DMA((count,))]
    return call(
        functools.partial(pack_kernel, plan),
        "pack",
        [SCALAR, SLOW, FAST, pl.BlockSpec(memory_space=pl.ANY)],
        shapes,
        scratch,
        1000,
        info,
        source,
        conductance,
        token,
    )


def join_kernel(start, own, other, out):
    size = own.shape[0]
    out[:size] = own[...]
    out[size:] = other[start : start + size]


def join(own, other, start):
    shape = (2 * own.shape[0],) + own.shape[1:]
    out_shape = jax.ShapeDtypeStruct(shape, own.dtype)
    kernel = functools.partial(join_kernel, start)
    return call(kernel, "join", [FAST] * 2, out_shape, [], 1000, own, other)


def along_z(rows, band):
    high = rows.astype(jnp.bfloat16)
    low = (rows - high.astype(jnp.float32)).astype(jnp.bfloat16)
    both = jnp.concatenate([high, low], axis=1)
    return jnp.dot(both, band[...], preferred_element_type=jnp.float32)


def sweep_kernel(adjoint, layout, begin, lead, place, *refs):
    planes = GROUP + 2 * HALO
    arrays = 1 + max(number for number, _ in layout)
    sources = [(refs[number], offset) for number, offset in layout]
    shift, band = refs[arrays], refs[arrays + 1]
    if lead is None:
        cond, out = refs[arrays + 2], refs[arrays + 3]
    else:
        out, cond = refs[arrays + 2], refs[arrays + 3]
    inverse, flat, start, gain, first, lateral = refs[-6:]
    _, width_y, step, width_z = start.shape
    count = out.shape[0]

    if adjoint:
        inverse[...] = 1.0 / cond[HALO : planes - HALO]
    if lead is not None:
        for slot, (source, offset) in enumerate(sources):
            terms = [source[offset + lead + i].astype(jnp.float32) for i in range(3)]
            cond[place[slot]] = (terms[0] + terms[1]) + terms[2]

    def relax(old, low, high, put):
        for plane in range(low, high):
            rows = old[plane].reshape(width_y * step, width_z)
            lateral[...] = along_z(rows, band).reshape(width_y, step, width_z)
            for y in range(width_y):
                total = old[plane - 1, y] + old[plane + 1, y]
                if y > 0:
                    total = total + old[plane, y - 1]
                if y < width_y - 1:
                    total = total + old[plane, y + 1]
                put(plane, y, start[plane, y] + gain[plane, y] * (total + lateral[y]))

    def keep(plane, y, state):
        first[plane, y] = state

    def one_pass(number, carry):
        at = pl.multiple_of(number * step, step)
        level = shift[pl.ds(begin + at, step), :]
        for slot, (source, offset) in enumerate(sources):
            plane = place[slot]
            piece = source[pl.ds(offset + begin + at, step)].astype(jnp.float32)
            flat[slot] = piece.reshape(step * width_y, width_z)
            for y in range(width_y):
                coeff = cond[plane, pl.ds(y, 1), :]
                diag = level + 6.0 * coeff
                guess = pltpu.reciprocal(diag, approx=True)
                recip = guess * (2.0 - diag * guess)
                scaled = recip * coeff
                force = flat[slot, pl.ds(y, step, stride=width_y), :]
                gain[plane, y] = scaled
                start[plane, y] = force * (scaled if adjoint else recip)

        def emit(plane, y, state):
            if adjoint:
                state = state * inverse[plane - HALO, pl.ds(y, 1), :]
            spot = ((plane - HALO) * width_y + y) * width_z
            out[pl.ds(at, step), spot : spot + width_z] = state.astype(jnp.bfloat16)

        relax(start, 1, planes - 1, keep)
        relax(first, HALO, planes - HALO, emit)
        return carry

    lax.fori_loop(0, count // step, one_pass, 0)


def sweep(adjoint, place, sources, shift, band, cond, span=None):
    width_z = shift.shape[1]
    begin, count = span or (0, shift.shape[0])
    size = sources[0].shape[0] // 2
    layout = [(i, at) for i, array in enumerate(sources) for at in range(0, array.shape[0], size)]
    width_y = sources[0].shape[1]
    planes = GROUP + 2 * HALO
    step = STEP if count % STEP == 0 else STEP // 2
    cells = GROUP * width_y * width_z
    out_shape = [jax.ShapeDtypeStruct((count, cells), jnp.bfloat16)]
    if cond is None:
        out_shape += [jax.ShapeDtypeStruct((planes, width_y, width_z), jnp.float32)]
    field = pltpu.VMEM((planes, width_y, step, width_z), jnp.float32)
    scratch = [
        pltpu.VMEM((GROUP, width_y, width_z), jnp.float32),
        pltpu.VMEM((planes, step * width_y, width_z), jnp.float32),
        field,
        field,
        field,
        pltpu.VMEM((width_y, step, width_z), jnp.float32),
    ]
    operands = [place, *sources, shift, band] + ([] if cond is None else [cond])
    return call(
        functools.partial(sweep_kernel, adjoint, layout, begin, shift.shape[0] if cond is None else None),
        "adjoint_sweeps" if adjoint else "direct_sweeps",
        [SCALAR] + [FAST] * (len(operands) - 1),
        out_shape,
        scratch,
        SWEEP_COST * count * cells,
        *operands,
    )


def scaled_factors(factors, singular):
    return (factors * (1.0 / jnp.sqrt(singular[...]))).astype(jnp.bfloat16)


def slab(refs, at, depth):
    span = pl.ds(pl.multiple_of(at, 128), depth)
    return jnp.concatenate([ref[:, span] for ref in refs], axis=0)


def gram_kernel(start, chunks, parts, shares, last, info, factors, singular, *refs):
    own, far, direct = refs[:chunks], refs[chunks : 2 * chunks], refs[2 * chunks : 2 * chunks + parts]
    rest = refs[2 * chunks + parts :]
    if last:
        older, older_modes = rest[:2]
        rest = rest[2:]
        kept, sent, kept_modes, sent_modes = rest[0], rest[1:-4], rest[-4], rest[-3]
    pieces, modes = rest[-2:]
    member, core, share = info[0], info[1], info[2]
    adjoint = [ref for pair in zip(own, far) for ref in pair]
    rows_total, cells = sum(ref.shape[0] for ref in adjoint), own[0].shape[1]
    count, width, _ = pieces.shape
    depth = cells // GROUP
    dims = (((1,), (1,)), ((), ()))
    total = jnp.zeros((count * width, rows_total), jnp.float32)
    for plane in range(GROUP):
        rows, cols = slab(adjoint, plane * depth, depth), slab(direct, plane * depth, depth)
        total = total + lax.dot_general(cols, rows, dims, preferred_element_type=jnp.float32)
    per_share = factors.shape[1] // shares
    window = factors[:, pl.ds(pl.multiple_of(share * per_share, per_share), per_share)]
    window = scaled_factors(window[:, start : start + rows_total], singular)

    def by_half(mine, other):
        return [jnp.where(core == 0, mine, other), jnp.where(core == 0, other, mine)]

    left, ordered, at = [], [], 0
    for ref in own:
        middle, end = at + ref.shape[0], at + 2 * ref.shape[0]
        left += by_half(window[:, at:middle], window[:, middle:end])
        ordered += by_half(total[:, at:middle], total[:, middle:end])
        at = end
    ordered = jnp.concatenate(ordered, axis=1)
    for part in range(count):
        pieces[part] = ordered[part * width : (part + 1) * width]
    term = jnp.dot(
        jnp.concatenate(left, axis=1), slab(adjoint, member * depth, depth), preferred_element_type=jnp.float32
    )
    if not last:
        modes[...] = term
        return
    modes[...] = older_modes[...] + term
    for number in range(len(sent) + 1):
        index = info[4 + number]
        if number == 0:
            kept[:, 0:start] = older[index]
            kept[:, start:] = pieces[index]
        else:
            sent[number - 1][:, 0:start] = older[index].astype(jnp.bfloat16)
            sent[number - 1][:, start:] = pieces[index].astype(jnp.bfloat16)
    wide = depth // shares
    for step in range(shares):
        piece = modes[:, pl.ds(pl.multiple_of(((share + step) % shares) * wide, wide), wide)]
        if step == 0:
            kept_modes[...] = piece
        else:
            sent_modes[step - 1] = piece.astype(jnp.bfloat16)


def gram_part(info, start, own, far, factors, singular, direct, blocks, older, layers):
    cells = own[0].shape[1]
    width = direct[0].shape[0]
    shares = len(direct) // blocks
    mode_count, rows = factors.shape[0], factors.shape[1] // shares
    depth = cells // GROUP
    height = 2 * sum(a.shape[0] for a in own)
    pieces = (shares * blocks, width, height)
    operands = [info, factors, singular, *own, *far, *direct]
    if older is None:
        out_shape = [
            jax.ShapeDtypeStruct(pieces, jnp.float32),
            jax.ShapeDtypeStruct((mode_count, depth), jnp.float32),
        ]
        scratch = []
    else:
        operands += older
        out_shape = [jax.ShapeDtypeStruct((width, rows), jnp.float32)]
        out_shape += [jax.ShapeDtypeStruct((width, rows), jnp.bfloat16)] * (layers - 1)
        out_shape += [
            jax.ShapeDtypeStruct((mode_count, depth // shares), jnp.float32),
            jax.ShapeDtypeStruct((shares - 1, mode_count, depth // shares), jnp.bfloat16),
        ]
        scratch = [pltpu.VMEM(pieces, jnp.float32), pltpu.VMEM((mode_count, depth), jnp.float32)]
    return call(
        functools.partial(gram_kernel, start, len(own), len(direct), shares, older is not None),
        "gram_part",
        [SCALAR] + [FAST] * (len(operands) - 1),
        out_shape,
        scratch,
        height * cells,
        *operands,
    )


def modes_kernel(parts, shares, info, factors, singular, *refs):
    direct, kept, sent = refs[:parts], refs[parts], refs[parts + 1 :]
    member, share = info[0], info[2]
    depth = direct[0].shape[1] // GROUP
    wide = depth // shares
    width = direct[0].shape[0]
    blocks = parts // shares

    def columns(owner, number):
        base = (owner * blocks + number) * GROUP * width
        spans = [factors[:, base + i * width : base + (i + 1) * width] for i in range(GROUP)]
        return sum(jnp.where(member == i, span, 0.0) for i, span in enumerate(spans))

    right = []
    for part in range(parts):
        owner = (share + shares - part // blocks) % shares
        right.append(sum(jnp.where(owner == i, columns(i, part % blocks), 0.0) for i in range(shares)))
    right = scaled_factors(jnp.concatenate(right, axis=1), singular)
    for mask in range(GROUP):
        at = (member ^ mask) * depth + share * wide
        term = jnp.dot(right, slab(direct, at, wide), preferred_element_type=jnp.float32)
        if mask == 0:
            kept[...] = term
        else:
            sent[mask - 1][...] = term.astype(jnp.bfloat16)


def direct_part(info, factors, singular, direct, shares):
    width, cells = direct[0].shape
    shape = (factors.shape[0], cells // GROUP // shares)
    operands = [info, factors, singular, *direct]
    return call(
        functools.partial(modes_kernel, len(direct), shares),
        "direct_modes_part",
        [SCALAR] + [FAST] * (len(operands) - 1),
        [jax.ShapeDtypeStruct(shape, jnp.float32)] + [jax.ShapeDtypeStruct(shape, jnp.bfloat16)] * (GROUP - 1),
        [],
        width * cells,
        *operands,
    )


def band_matrix(width):
    near = (jnp.abs(jnp.arange(width)[:, None] - jnp.arange(width)[None, :]) == 1).astype(jnp.bfloat16)
    return jnp.concatenate([near, near])


def lookup(indices, shift_list):
    levels = jnp.arange(shift_list.shape[0], dtype=jnp.int32)
    picked = jnp.where(indices[:, None] == levels[None, :], shift_list[None, :], jnp.float32(0.0))
    return jnp.sum(picked, axis=1)


def pick(array, index, axis=0):
    return lax.dynamic_index_in_dim(array, index, axis, keepdims=False)


def after(array, *others):
    return lax.optimization_barrier((array, *others))[0]


def per_device(
    forcing_direct,
    forcing_adjoint,
    conductance,
    shift_table,
    freq_direct,
    freq_adjoint,
    left_factors,
    right_factors,
    singular_values,
):
    n_space, n_snap = lax.axis_size("space"), lax.axis_size("snap")
    rows, plane_x, width_y, width_z = forcing_direct.shape
    layers = n_space // GROUP
    block = rows * n_snap // n_space
    blocks = rows // (GROUP * block)
    mode_count = left_factors.shape[1]
    rows_y = width_y // n_snap
    weight = 1.0 / math.sqrt(plane_x * n_space * width_y * width_z)

    spot, share = lax.axis_index("space"), lax.axis_index("snap")
    layer, member = spot // GROUP, spot % GROUP
    core, high = member % 2, member // 2

    def piece_index(target):
        return ((share - target // blocks) % n_snap) * blocks + target % blocks

    info = jnp.stack(
        [member, core, share, layer] + [piece_index((layer + step) % layers) for step in range(layers)]
    ).astype(jnp.int32)

    def swap(array, mask):
        return lax.ppermute(array, "space", [(i, i ^ mask) for i in range(n_space)])

    def around(array, step):
        return lax.ppermute(array, "snap", [(i, (i + step) % n_snap) for i in range(n_snap)])

    ups = [(i, i + GROUP) for i in range(n_space - GROUP)]
    downs = [(i + GROUP, i) for i in range(n_space - GROUP)]
    upper = lambda pairs, wanted: [p for p in pairs if (p[0] % GROUP) // 2 == wanted]
    early = lambda array: lax.ppermute(array, "space", upper(ups, 1) + upper(downs, 0))
    late = lambda array: lax.ppermute(array, "space", upper(ups, 0) + upper(downs, 1))

    sizes = [rows * part // sum(CHUNKS) // 32 * 16 for part in CHUNKS[1:]]
    sizes = [rows // 2 - sum(sizes)] + sizes
    starts = [2 * sum(sizes[:i]) for i in range(len(sizes))]
    sets = forcing_direct.reshape(blocks, GROUP, block, width_y, width_z)
    rows_adj = forcing_adjoint.reshape(rows, width_y, width_z)
    own = lambda i: ("half", starts[i], sizes[i], False)
    cross = lambda i: ("half", starts[i], sizes[i], True)
    near_d, far_d, cross_d, own_d = pack(info, sets, conductance, info, [[("set", mask)] for mask in (2, 3, 1, 0)])
    crossed_d = swap(cross_d, 1)
    to_core, *own_adj = pack(
        info,
        rows_adj,
        conductance,
        crossed_d,
        [[cross(i) for i in range(len(sizes))]] + [[own(i)] for i in range(len(sizes))],
    )

    wide = lambda values: jnp.broadcast_to(values[:, None], (values.shape[0], width_z))
    dir_levels = lookup(freq_direct, shift_table).reshape(blocks, GROUP, block)
    dir_shift = wide(pick(dir_levels, member, 1).reshape(-1))
    adj_levels = lookup(freq_adjoint, shift_table)
    adj_shift = [
        wide(lax.dynamic_slice_in_dim(adj_levels, at + core * size, size, 0)) for at, size in zip(starts, sizes)
    ]
    inside = lambda index: HALO + index
    below = lambda index: index - HALO
    above = lambda index: index + GROUP + HALO
    place = jnp.stack(
        [inside(member ^ k) for k in range(4)]
        + [jnp.where(high == 1, below(member ^ k), above(member ^ k)) for k in (0, 1)]
        + [jnp.where(high == 1, above(member ^ k), below(member ^ k)) for k in (2, 3)]
    ).astype(jnp.int32)
    band = band_matrix(width_z)

    near, far = swap(near_d, 2), swap(far_d, 3)
    crossed = swap(to_core, 1)
    pair_d = join(own_d, crossed_d, 0)
    spots = [sum(sizes[:i]) for i in range(len(sizes))]
    pairs = [join(own, crossed, at) for own, at in zip(own_adj, spots)]
    e_d = early(pair_d)
    late_near, late_far = late(near), late(far)
    sources = [pair_d, near, far, e_d, late_near, late_far]
    dir_state, cond = sweep(False, place, sources, dir_shift, band, None, (0, block))
    dir_states = [dir_state] + [
        sweep(False, place, sources, dir_shift, band, cond, (i * block, block))[0] for i in range(1, blocks)
    ]
    moved = [[around(state, step) for state in dir_states] for step in range(1, n_snap)]
    everyone = dir_states + [state for states in moved for state in states]
    y_adj, e_adj, l_adj, own_states, far_states = [], [], [], [], []
    for i, pair in enumerate(pairs):
        y_after = [near, far, late_near] if i == 0 else [y_adj[-1], dir_states[0]]
        e_after = [e_d] if i == 0 else [e_adj[-1], dir_states[-1]]
        y_adj.append(swap(after(pair, *y_after), 2))
        e_adj.append(early(after(pair, *e_after)))
        l_adj.append(late(after(y_adj[i], l_adj[-1]) if i else y_adj[i]))
        arrived = after(y_adj[i], everyone[blocks]) if i == 1 else y_adj[i]
        if i == 2:
            arrived = after(y_adj[i], everyone[-1])
        sources = [pair, arrived, e_adj[i], l_adj[i]]
        own_states.append(sweep(True, place, sources, adj_shift[i], band, cond)[0])
        far_states.append(swap(own_states[i], 1))

    singular = singular_values.reshape(1, mode_count).T
    left, right = left_factors.T, right_factors.T
    kept, *sent = direct_part(info, right, singular, everyone, n_snap)
    for mask in range(1, GROUP):
        kept = kept + swap(sent[mask - 1], mask).astype(jnp.float32)
    direct_modes = kept.reshape(mode_count, 1, rows_y, width_z)

    outs = gram_part(
        info, 0, own_states[:-1], far_states[:-1], left, singular, everyone, blocks, None, layers
    )
    outs = gram_part(
        info, starts[-1], own_states[-1:], far_states[-1:], left, singular, everyone, blocks, list(outs), layers
    )
    kept, *sent, kept_modes, sent_modes = outs
    for step in range(1, layers):
        pairs = [(i, (i + GROUP * step) % n_space) for i in range(n_space)]
        kept = kept + lax.ppermute(sent[step - 1], "space", pairs).astype(jnp.float32)
    gram = (kept * weight).T
    for step in range(1, n_snap):
        kept_modes = kept_modes + around(sent_modes[step - 1], step).astype(jnp.float32)
    adjoint_modes = kept_modes.reshape(mode_count, 1, rows_y, width_z)
    return (gram, direct_modes, adjoint_modes)


def solution(mesh):
    placed = (
        P("snap", "space", None, None),
        P("snap", "space", None, None),
        P("space", None, None),
        P(),
        P("snap"),
        P("snap"),
        P(),
        P(),
        P(),
    )
    return jax.shard_map(
        per_device,
        mesh=mesh,
        in_specs=placed,
        out_specs=(
            P("snap", "space"),
            P(None, "space", "snap", None),
            P(None, "space", "snap", None),
        ),
        check_vma=False,
    )
```

```python
import functools
import math

import jax
import jax.numpy as jnp
from jax import lax
from jax.experimental import pallas as pl
from jax.experimental.pallas import tpu as pltpu
from jax.sharding import PartitionSpec as P

GROUP = 4
HALO = 2
STEP = 32
SWEEP_COST = 6500
CHUNKS = (3, 3, 2)
EXTRA = 4
VMEM = 20 * 1024 * 1024

SLOW = pl.BlockSpec(memory_space=pltpu.HBM)
FAST = pl.BlockSpec(memory_space=pltpu.VMEM)
SCALAR = pl.BlockSpec(memory_space=pltpu.SMEM)


def call(kernel, name, in_specs, out_shape, scratch, flops, *operands):
    return pl.pallas_call(
        kernel,
        in_specs=in_specs,
        out_specs=jax.tree.map(lambda _: FAST, out_shape),
        out_shape=out_shape,
        scratch_shapes=scratch,
        compiler_params=pltpu.CompilerParams(vmem_limit_bytes=VMEM),
        cost_estimate=pl.CostEstimate(flops=flops, bytes_accessed=1024, transcendentals=0),
        name=name,
    )(*operands)


def pack_kernel(plan, info, source, conductance, token, *refs):
    outs, field, sems = refs[:-2], refs[-2], refs[-1]
    member, core = info[0], info[1]
    copies, more = [], []
    values = conductance[0]
    high = values.astype(jnp.bfloat16)
    rest = values - high.astype(jnp.float32)
    middle = rest.astype(jnp.bfloat16)

    def add(group, source, target):
        copy = pltpu.make_async_copy(source, target, sems.at[len(copies) + len(more)])
        group.append(copy)

    for out, pieces in zip(outs, plan):
        at = 0
        for kind, *what in pieces:
            if kind == "set":
                blocks, _, block = source.shape[:3]
                for i in range(blocks):
                    add(copies, source.at[i, member ^ what[0]], out.at[pl.ds(at + i * block, block)])
                at += blocks * block
                add(more, field, out.at[pl.ds(at, EXTRA)])
                at += EXTRA
            else:
                start, size, flip = what
                spot = start + (1 - core if flip else core) * size
                add(copies, source.at[pl.ds(spot, size)], out.at[pl.ds(at, size)])
                at += size
    for copy in copies:
        copy.start()
    field[0] = high
    field[1] = middle
    field[2] = (rest - middle.astype(jnp.float32)).astype(jnp.bfloat16)
    field[3] = jnp.zeros_like(high)
    for copy in more:
        copy.start()
    for copy in copies + more:
        copy.wait()


def pack(info, source, conductance, token, plan):
    blocks, block = source.shape[0], source.shape[2]
    width_y, width_z = source.shape[-2:]
    lengths = {"set": lambda what: blocks * block + EXTRA, "half": lambda what: what[1]}
    shapes, count = [], 0
    for pieces in plan:
        entries = sum(lengths[kind](what) for kind, *what in pieces)
        shapes.append(jax.ShapeDtypeStruct((entries, width_y, width_z), source.dtype))
        count += sum(blocks + 1 if piece[0] == "set" else 1 for piece in pieces)
    scratch = [pltpu.VMEM((EXTRA, width_y, width_z), source.dtype), pltpu.SemaphoreType.DMA((count,))]
    return call(
        functools.partial(pack_kernel, plan),
        "pack",
        [SCALAR, SLOW, FAST, pl.BlockSpec(memory_space=pl.ANY)],
        shapes,
        scratch,
        1000,
        info,
        source,
        conductance,
        token,
    )


def join_kernel(start, own, other, out):
    size = own.shape[0]
    out[:size] = own[...]
    out[size:] = other[start : start + size]


def join(own, other, start):
    shape = (2 * own.shape[0],) + own.shape[1:]
    out_shape = jax.ShapeDtypeStruct(shape, own.dtype)
    kernel = functools.partial(join_kernel, start)
    return call(kernel, "join", [FAST] * 2, out_shape, [], 1000, own, other)


def along_z(rows, band):
    high = rows.astype(jnp.bfloat16)
    low = (rows - high.astype(jnp.float32)).astype(jnp.bfloat16)
    both = jnp.concatenate([high, low], axis=1)
    return jnp.dot(both, band[...], preferred_element_type=jnp.float32)


def sweep_kernel(adjoint, layout, begin, lead, place, *refs):
    planes = GROUP + 2 * HALO
    arrays = 1 + max(number for number, _ in layout)
    sources = [(refs[number], offset) for number, offset in layout]
    shift, band = refs[arrays], refs[arrays + 1]
    if lead is None:
        cond, out = refs[arrays + 2], refs[arrays + 3]
    else:
        out, cond = refs[arrays + 2], refs[arrays + 3]
    inverse, flat, start, gain, first, lateral = refs[-6:]
    _, width_y, step, width_z = start.shape
    count = out.shape[0]

    if adjoint:
        inverse[...] = 1.0 / cond[HALO : planes - HALO]
    if lead is not None:
        for slot, (source, offset) in enumerate(sources):
            terms = [source[offset + lead + i].astype(jnp.float32) for i in range(3)]
            cond[place[slot]] = (terms[0] + terms[1]) + terms[2]

    def relax(old, low, high, put):
        for plane in range(low, high):
            rows = old[plane].reshape(width_y * step, width_z)
            lateral[...] = along_z(rows, band).reshape(width_y, step, width_z)
            for y in range(width_y):
                total = old[plane - 1, y] + old[plane + 1, y]
                if y > 0:
                    total = total + old[plane, y - 1]
                if y < width_y - 1:
                    total = total + old[plane, y + 1]
                put(plane, y, start[plane, y] + gain[plane, y] * (total + lateral[y]))

    def keep(plane, y, state):
        first[plane, y] = state

    def one_pass(number, carry):
        at = pl.multiple_of(number * step, step)
        level = shift[pl.ds(begin + at, step), :]
        for slot, (source, offset) in enumerate(sources):
            plane = place[slot]
            piece = source[pl.ds(offset + begin + at, step)].astype(jnp.float32)
            flat[slot] = piece.reshape(step * width_y, width_z)
            for y in range(width_y):
                coeff = cond[plane, pl.ds(y, 1), :]
                diag = level + 6.0 * coeff
                recip = pltpu.reciprocal(diag, approx=True)
                scaled = recip * coeff
                force = flat[slot, pl.ds(y, step, stride=width_y), :]
                gain[plane, y] = scaled
                start[plane, y] = force * (scaled if adjoint else recip)

        def emit(plane, y, state):
            if adjoint:
                state = state * inverse[plane - HALO, pl.ds(y, 1), :]
            spot = ((plane - HALO) * width_y + y) * width_z
            out[pl.ds(at, step), spot : spot + width_z] = state.astype(jnp.bfloat16)

        relax(start, 1, planes - 1, keep)
        relax(first, HALO, planes - HALO, emit)
        return carry

    lax.fori_loop(0, count // step, one_pass, 0)


def sweep(adjoint, place, sources, shift, band, cond, span=None):
    width_z = shift.shape[1]
    begin, count = span or (0, shift.shape[0])
    size = sources[0].shape[0] // 2
    layout = [(i, at) for i, array in enumerate(sources) for at in range(0, array.shape[0], size)]
    width_y = sources[0].shape[1]
    planes = GROUP + 2 * HALO
    step = STEP if count % STEP == 0 else STEP // 2
    cells = GROUP * width_y * width_z
    out_shape = [jax.ShapeDtypeStruct((count, cells), jnp.bfloat16)]
    if cond is None:
        out_shape += [jax.ShapeDtypeStruct((planes, width_y, width_z), jnp.float32)]
    field = pltpu.VMEM((planes, width_y, step, width_z), jnp.float32)
    scratch = [
        pltpu.VMEM((GROUP, width_y, width_z), jnp.float32),
        pltpu.VMEM((planes, step * width_y, width_z), jnp.float32),
        field,
        field,
        field,
        pltpu.VMEM((width_y, step, width_z), jnp.float32),
    ]
    operands = [place, *sources, shift, band] + ([] if cond is None else [cond])
    return call(
        functools.partial(sweep_kernel, adjoint, layout, begin, shift.shape[0] if cond is None else None),
        "adjoint_sweeps" if adjoint else "direct_sweeps",
        [SCALAR] + [FAST] * (len(operands) - 1),
        out_shape,
        scratch,
        SWEEP_COST * count * cells,
        *operands,
    )


def scaled_factors(factors, singular):
    return (factors * (1.0 / jnp.sqrt(singular[...]))).astype(jnp.bfloat16)


def slab(refs, at, depth):
    span = pl.ds(pl.multiple_of(at, 128), depth)
    return jnp.concatenate([ref[:, span] for ref in refs], axis=0)


def gram_kernel(start, chunks, parts, shares, last, info, factors, singular, *refs):
    own, far, direct = refs[:chunks], refs[chunks : 2 * chunks], refs[2 * chunks : 2 * chunks + parts]
    rest = refs[2 * chunks + parts :]
    if last:
        older, older_modes = rest[:2]
        rest = rest[2:]
        kept, sent, kept_modes, sent_modes = rest[0], rest[1:-4], rest[-4], rest[-3]
    pieces, modes = rest[-2:]
    member, core, share = info[0], info[1], info[2]
    adjoint = [ref for pair in zip(own, far) for ref in pair]
    rows_total, cells = sum(ref.shape[0] for ref in adjoint), own[0].shape[1]
    count, width, _ = pieces.shape
    depth = cells // GROUP
    dims = (((1,), (1,)), ((), ()))
    total = jnp.zeros((count * width, rows_total), jnp.float32)
    for plane in range(GROUP):
        rows, cols = slab(adjoint, plane * depth, depth), slab(direct, plane * depth, depth)
        total = total + lax.dot_general(cols, rows, dims, preferred_element_type=jnp.float32)
    per_share = factors.shape[1] // shares
    window = factors[:, pl.ds(pl.multiple_of(share * per_share, per_share), per_share)]
    window = scaled_factors(window[:, start : start + rows_total], singular)

    def by_half(mine, other):
        return [jnp.where(core == 0, mine, other), jnp.where(core == 0, other, mine)]

    left, ordered, at = [], [], 0
    for ref in own:
        middle, end = at + ref.shape[0], at + 2 * ref.shape[0]
        left += by_half(window[:, at:middle], window[:, middle:end])
        ordered += by_half(total[:, at:middle], total[:, middle:end])
        at = end
    ordered = jnp.concatenate(ordered, axis=1)
    for part in range(count):
        pieces[part] = ordered[part * width : (part + 1) * width]
    term = jnp.dot(
        jnp.concatenate(left, axis=1), slab(adjoint, member * depth, depth), preferred_element_type=jnp.float32
    )
    if not last:
        modes[...] = term
        return
    modes[...] = older_modes[...] + term
    for number in range(len(sent) + 1):
        index = info[4 + number]
        if number == 0:
            kept[:, 0:start] = older[index]
            kept[:, start:] = pieces[index]
        else:
            sent[number - 1][:, 0:start] = older[index].astype(jnp.bfloat16)
            sent[number - 1][:, start:] = pieces[index].astype(jnp.bfloat16)
    wide = depth // shares
    for step in range(shares):
        piece = modes[:, pl.ds(pl.multiple_of(((share + step) % shares) * wide, wide), wide)]
        if step == 0:
            kept_modes[...] = piece
        else:
            sent_modes[step - 1] = piece.astype(jnp.bfloat16)


def gram_part(info, start, own, far, factors, singular, direct, blocks, older, layers):
    cells = own[0].shape[1]
    width = direct[0].shape[0]
    shares = len(direct) // blocks
    mode_count, rows = factors.shape[0], factors.shape[1] // shares
    depth = cells // GROUP
    height = 2 * sum(a.shape[0] for a in own)
    pieces = (shares * blocks, width, height)
    operands = [info, factors, singular, *own, *far, *direct]
    if older is None:
        out_shape = [
            jax.ShapeDtypeStruct(pieces, jnp.float32),
            jax.ShapeDtypeStruct((mode_count, depth), jnp.float32),
        ]
        scratch = []
    else:
        operands += older
        out_shape = [jax.ShapeDtypeStruct((width, rows), jnp.float32)]
        out_shape += [jax.ShapeDtypeStruct((width, rows), jnp.bfloat16)] * (layers - 1)
        out_shape += [
            jax.ShapeDtypeStruct((mode_count, depth // shares), jnp.float32),
            jax.ShapeDtypeStruct((shares - 1, mode_count, depth // shares), jnp.bfloat16),
        ]
        scratch = [pltpu.VMEM(pieces, jnp.float32), pltpu.VMEM((mode_count, depth), jnp.float32)]
    return call(
        functools.partial(gram_kernel, start, len(own), len(direct), shares, older is not None),
        "gram_part",
        [SCALAR] + [FAST] * (len(operands) - 1),
        out_shape,
        scratch,
        height * cells,
        *operands,
    )


def modes_kernel(parts, shares, info, factors, singular, *refs):
    direct, kept, sent = refs[:parts], refs[parts], refs[parts + 1 :]
    member, share = info[0], info[2]
    depth = direct[0].shape[1] // GROUP
    wide = depth // shares
    width = direct[0].shape[0]
    blocks = parts // shares

    def columns(owner, number):
        base = (owner * blocks + number) * GROUP * width
        spans = [factors[:, base + i * width : base + (i + 1) * width] for i in range(GROUP)]
        return sum(jnp.where(member == i, span, 0.0) for i, span in enumerate(spans))

    right = []
    for part in range(parts):
        owner = (share + shares - part // blocks) % shares
        right.append(sum(jnp.where(owner == i, columns(i, part % blocks), 0.0) for i in range(shares)))
    right = scaled_factors(jnp.concatenate(right, axis=1), singular)
    for mask in range(GROUP):
        at = (member ^ mask) * depth + share * wide
        term = jnp.dot(right, slab(direct, at, wide), preferred_element_type=jnp.float32)
        if mask == 0:
            kept[...] = term
        else:
            sent[mask - 1][...] = term.astype(jnp.bfloat16)


def direct_part(info, factors, singular, direct, shares):
    width, cells = direct[0].shape
    shape = (factors.shape[0], cells // GROUP // shares)
    operands = [info, factors, singular, *direct]
    return call(
        functools.partial(modes_kernel, len(direct), shares),
        "direct_modes_part",
        [SCALAR] + [FAST] * (len(operands) - 1),
        [jax.ShapeDtypeStruct(shape, jnp.float32)] + [jax.ShapeDtypeStruct(shape, jnp.bfloat16)] * (GROUP - 1),
        [],
        width * cells,
        *operands,
    )


def band_matrix(width):
    near = (jnp.abs(jnp.arange(width)[:, None] - jnp.arange(width)[None, :]) == 1).astype(jnp.bfloat16)
    return jnp.concatenate([near, near])


def lookup(indices, shift_list):
    levels = jnp.arange(shift_list.shape[0], dtype=jnp.int32)
    picked = jnp.where(indices[:, None] == levels[None, :], shift_list[None, :], jnp.float32(0.0))
    return jnp.sum(picked, axis=1)


def pick(array, index, axis=0):
    return lax.dynamic_index_in_dim(array, index, axis, keepdims=False)


def after(array, *others):
    return lax.optimization_barrier((array, *others))[0]


def per_device(
    forcing_direct,
    forcing_adjoint,
    conductance,
    shift_table,
    freq_direct,
    freq_adjoint,
    left_factors,
    right_factors,
    singular_values,
):
    n_space, n_snap = lax.axis_size("space"), lax.axis_size("snap")
    rows, plane_x, width_y, width_z = forcing_direct.shape
    layers = n_space // GROUP
    block = rows * n_snap // n_space
    blocks = rows // (GROUP * block)
    mode_count = left_factors.shape[1]
    rows_y = width_y // n_snap
    weight = 1.0 / math.sqrt(plane_x * n_space * width_y * width_z)

    spot, share = lax.axis_index("space"), lax.axis_index("snap")
    layer, member = spot // GROUP, spot % GROUP
    core, high = member % 2, member // 2

    def piece_index(target):
        return ((share - target // blocks) % n_snap) * blocks + target % blocks

    info = jnp.stack(
        [member, core, share, layer] + [piece_index((layer + step) % layers) for step in range(layers)]
    ).astype(jnp.int32)

    def swap(array, mask):
        return lax.ppermute(array, "space", [(i, i ^ mask) for i in range(n_space)])

    def around(array, step):
        return lax.ppermute(array, "snap", [(i, (i + step) % n_snap) for i in range(n_snap)])

    ups = [(i, i + GROUP) for i in range(n_space - GROUP)]
    downs = [(i + GROUP, i) for i in range(n_space - GROUP)]
    upper = lambda pairs, wanted: [p for p in pairs if (p[0] % GROUP) // 2 == wanted]
    early = lambda array: lax.ppermute(array, "space", upper(ups, 1) + upper(downs, 0))
    late = lambda array: lax.ppermute(array, "space", upper(ups, 0) + upper(downs, 1))

    sizes = [rows * part // sum(CHUNKS) // 32 * 16 for part in CHUNKS[1:]]
    sizes = [rows // 2 - sum(sizes)] + sizes
    starts = [2 * sum(sizes[:i]) for i in range(len(sizes))]
    sets = forcing_direct.reshape(blocks, GROUP, block, width_y, width_z)
    rows_adj = forcing_adjoint.reshape(rows, width_y, width_z)
    own = lambda i: ("half", starts[i], sizes[i], False)
    cross = lambda i: ("half", starts[i], sizes[i], True)
    near_d, far_d, cross_d, own_d = pack(info, sets, conductance, info, [[("set", mask)] for mask in (2, 3, 1, 0)])
    crossed_d = swap(cross_d, 1)
    to_core, *own_adj = pack(
        info,
        rows_adj,
        conductance,
        crossed_d,
        [[cross(i) for i in range(len(sizes))]] + [[own(i)] for i in range(len(sizes))],
    )

    wide = lambda values: jnp.broadcast_to(values[:, None], (values.shape[0], width_z))
    dir_levels = lookup(freq_direct, shift_table).reshape(blocks, GROUP, block)
    dir_shift = wide(pick(dir_levels, member, 1).reshape(-1))
    adj_levels = lookup(freq_adjoint, shift_table)
    adj_shift = [
        wide(lax.dynamic_slice_in_dim(adj_levels, at + core * size, size, 0)) for at, size in zip(starts, sizes)
    ]
    inside = lambda index: HALO + index
    below = lambda index: index - HALO
    above = lambda index: index + GROUP + HALO
    place = jnp.stack(
        [inside(member ^ k) for k in range(4)]
        + [jnp.where(high == 1, below(member ^ k), above(member ^ k)) for k in (0, 1)]
        + [jnp.where(high == 1, above(member ^ k), below(member ^ k)) for k in (2, 3)]
    ).astype(jnp.int32)
    band = band_matrix(width_z)

    near, far = swap(near_d, 2), swap(far_d, 3)
    crossed = swap(to_core, 1)
    pair_d = join(own_d, crossed_d, 0)
    spots = [sum(sizes[:i]) for i in range(len(sizes))]
    pairs = [join(own, crossed, at) for own, at in zip(own_adj, spots)]
    e_d = early(pair_d)
    late_near, late_far = late(near), late(far)
    sources = [pair_d, near, far, e_d, late_near, late_far]
    dir_state, cond = sweep(False, place, sources, dir_shift, band, None, (0, block))
    dir_states = [dir_state] + [
        sweep(False, place, sources, dir_shift, band, cond, (i * block, block))[0] for i in range(1, blocks)
    ]
    moved = [[around(state, step) for state in dir_states] for step in range(1, n_snap)]
    everyone = dir_states + [state for states in moved for state in states]
    singular = singular_values.reshape(1, mode_count).T
    left, right = left_factors.T, right_factors.T
    kept, *sent = direct_part(info, right, singular, everyone, n_snap)
    y_adj, e_adj, l_adj, own_states, far_states = [], [], [], [], []
    for i, pair in enumerate(pairs):
        y_after = [near, far, late_near] if i == 0 else [y_adj[-1], dir_states[0]]
        e_after = [e_d] if i == 0 else [e_adj[-1], dir_states[-1]]
        y_adj.append(swap(after(pair, *y_after), 2))
        e_adj.append(early(after(pair, *e_after)))
        l_adj.append(late(after(y_adj[i], l_adj[-1]) if i else y_adj[i]))
        arrived = after(y_adj[i], everyone[blocks]) if i == 1 else y_adj[i]
        if i == 2:
            arrived = after(y_adj[i], kept)
        sources = [pair, arrived, e_adj[i], l_adj[i]]
        own_states.append(sweep(True, place, sources, adj_shift[i], band, cond)[0])
        far_states.append(swap(own_states[i], 1))

    for mask in range(1, GROUP):
        kept = kept + swap(sent[mask - 1], mask).astype(jnp.float32)
    direct_modes = kept.reshape(mode_count, 1, rows_y, width_z)

    outs = gram_part(
        info, 0, own_states[:-1], far_states[:-1], left, singular, everyone, blocks, None, layers
    )
    outs = gram_part(
        info, starts[-1], own_states[-1:], far_states[-1:], left, singular, everyone, blocks, list(outs), layers
    )
    kept, *sent, kept_modes, sent_modes = outs
    for step in range(1, layers):
        pairs = [(i, (i + GROUP * step) % n_space) for i in range(n_space)]
        kept = kept + lax.ppermute(sent[step - 1], "space", pairs).astype(jnp.float32)
    gram = (kept * weight).T
    for step in range(1, n_snap):
        kept_modes = kept_modes + around(sent_modes[step - 1], step).astype(jnp.float32)
    adjoint_modes = kept_modes.reshape(mode_count, 1, rows_y, width_z)
    return (gram, direct_modes, adjoint_modes)


def solution(mesh):
    placed = (
        P("snap", "space", None, None),
        P("snap", "space", None, None),
        P("space", None, None),
        P(),
        P("snap"),
        P("snap"),
        P(),
        P(),
        P(),
    )
    return jax.shard_map(
        per_device,
        mesh=mesh,
        in_specs=placed,
        out_specs=(
            P("snap", "space"),
            P(None, "space", "snap", None),
            P(None, "space", "snap", None),
        ),
        check_vma=False,
    )
```

```python
import functools
import math

import jax
import jax.numpy as jnp
from jax import lax
from jax.experimental import pallas as pl
from jax.experimental.pallas import tpu as pltpu
from jax.sharding import PartitionSpec as P

GROUP = 4
HALO = 2
STEP = 32
SWEEP_COST = 6500
CHUNKS = (3, 3, 2)
EXTRA = 4
VMEM = 20 * 1024 * 1024

SLOW = pl.BlockSpec(memory_space=pltpu.HBM)
FAST = pl.BlockSpec(memory_space=pltpu.VMEM)
SCALAR = pl.BlockSpec(memory_space=pltpu.SMEM)


def call(kernel, name, in_specs, out_shape, scratch, flops, *operands):
    return pl.pallas_call(
        kernel,
        in_specs=in_specs,
        out_specs=jax.tree.map(lambda _: FAST, out_shape),
        out_shape=out_shape,
        scratch_shapes=scratch,
        compiler_params=pltpu.CompilerParams(vmem_limit_bytes=VMEM),
        cost_estimate=pl.CostEstimate(flops=flops, bytes_accessed=1024, transcendentals=0),
        name=name,
    )(*operands)


def pack_kernel(plan, info, source, conductance, token, *refs):
    outs, field, sems = refs[:-2], refs[-2], refs[-1]
    member, core = info[0], info[1]
    copies, more = [], []
    values = conductance[0]
    high = values.astype(jnp.bfloat16)
    rest = values - high.astype(jnp.float32)
    middle = rest.astype(jnp.bfloat16)

    def add(group, source, target):
        copy = pltpu.make_async_copy(source, target, sems.at[len(copies) + len(more)])
        group.append(copy)

    for out, pieces in zip(outs, plan):
        at = 0
        for kind, *what in pieces:
            if kind == "set":
                blocks, _, block = source.shape[:3]
                for i in range(blocks):
                    add(copies, source.at[i, member ^ what[0]], out.at[pl.ds(at + i * block, block)])
                at += blocks * block
                add(more, field, out.at[pl.ds(at, EXTRA)])
                at += EXTRA
            else:
                start, size, flip = what
                spot = start + (1 - core if flip else core) * size
                add(copies, source.at[pl.ds(spot, size)], out.at[pl.ds(at, size)])
                at += size
    for copy in copies:
        copy.start()
    field[0] = high
    field[1] = middle
    field[2] = (rest - middle.astype(jnp.float32)).astype(jnp.bfloat16)
    field[3] = jnp.zeros_like(high)
    for copy in more:
        copy.start()
    for copy in copies + more:
        copy.wait()


def pack(info, source, conductance, token, plan):
    blocks, block = source.shape[0], source.shape[2]
    width_y, width_z = source.shape[-2:]
    lengths = {"set": lambda what: blocks * block + EXTRA, "half": lambda what: what[1]}
    shapes, count = [], 0
    for pieces in plan:
        entries = sum(lengths[kind](what) for kind, *what in pieces)
        shapes.append(jax.ShapeDtypeStruct((entries, width_y, width_z), source.dtype))
        count += sum(blocks + 1 if piece[0] == "set" else 1 for piece in pieces)
    scratch = [pltpu.VMEM((EXTRA, width_y, width_z), source.dtype), pltpu.SemaphoreType.DMA((count,))]
    return call(
        functools.partial(pack_kernel, plan),
        "pack",
        [SCALAR, SLOW, FAST, pl.BlockSpec(memory_space=pl.ANY)],
        shapes,
        scratch,
        1000,
        info,
        source,
        conductance,
        token,
    )


def join_kernel(start, own, other, out):
    size = own.shape[0]
    out[:size] = own[...]
    out[size:] = other[start : start + size]


def join(own, other, start):
    shape = (2 * own.shape[0],) + own.shape[1:]
    out_shape = jax.ShapeDtypeStruct(shape, own.dtype)
    kernel = functools.partial(join_kernel, start)
    return call(kernel, "join", [FAST] * 2, out_shape, [], 1000, own, other)


def along_z(rows, band):
    high = rows.astype(jnp.bfloat16)
    low = (rows - high.astype(jnp.float32)).astype(jnp.bfloat16)
    both = jnp.concatenate([high, low], axis=1)
    return jnp.dot(both, band[...], preferred_element_type=jnp.float32)


def sweep_kernel(adjoint, layout, begin, lead, place, *refs):
    planes = GROUP + 2 * HALO
    arrays = 1 + max(number for number, _ in layout)
    sources = [(refs[number], offset) for number, offset in layout]
    shift, band = refs[arrays], refs[arrays + 1]
    if lead is None:
        cond, out = refs[arrays + 2], refs[arrays + 3]
    else:
        out, cond = refs[arrays + 2], refs[arrays + 3]
    inverse, flat, start, gain, first, lateral = refs[-6:]
    _, width_y, step, width_z = start.shape
    count = out.shape[0]

    if adjoint:
        inverse[...] = 1.0 / cond[HALO : planes - HALO]
    if lead is not None:
        for slot, (source, offset) in enumerate(sources):
            terms = [source[offset + lead + i].astype(jnp.float32) for i in range(3)]
            cond[place[slot]] = (terms[0] + terms[1]) + terms[2]

    def relax(old, low, high, put):
        for plane in range(low, high):
            rows = old[plane].reshape(width_y * step, width_z)
            lateral[...] = along_z(rows, band).reshape(width_y, step, width_z)
            for y in range(width_y):
                total = old[plane - 1, y] + old[plane + 1, y]
                if y > 0:
                    total = total + old[plane, y - 1]
                if y < width_y - 1:
                    total = total + old[plane, y + 1]
                put(plane, y, start[plane, y] + gain[plane, y] * (total + lateral[y]))

    def keep(plane, y, state):
        first[plane, y] = state

    def one_pass(number, carry):
        at = pl.multiple_of(number * step, step)
        level = shift[pl.ds(begin + at, step), :]
        for slot, (source, offset) in enumerate(sources):
            plane = place[slot]
            piece = source[pl.ds(offset + begin + at, step)].astype(jnp.float32)
            flat[slot] = piece.reshape(step * width_y, width_z)
            for y in range(width_y):
                coeff = cond[plane, pl.ds(y, 1), :]
                diag = level + 6.0 * coeff
                recip = pltpu.reciprocal(diag, approx=True)
                scaled = recip * coeff
                force = flat[slot, pl.ds(y, step, stride=width_y), :]
                gain[plane, y] = scaled
                start[plane, y] = force * (scaled if adjoint else recip)

        def emit(plane, y, state):
            if adjoint:
                state = state * inverse[plane - HALO, pl.ds(y, 1), :]
            spot = ((plane - HALO) * width_y + y) * width_z
            out[pl.ds(at, step), spot : spot + width_z] = state.astype(jnp.bfloat16)

        relax(start, 1, planes - 1, keep)
        relax(first, HALO, planes - HALO, emit)
        return carry

    lax.fori_loop(0, count // step, one_pass, 0)


def sweep(adjoint, place, sources, shift, band, cond, span=None):
    width_z = shift.shape[1]
    begin, count = span or (0, shift.shape[0])
    size = sources[0].shape[0] // 2
    layout = [(i, at) for i, array in enumerate(sources) for at in range(0, array.shape[0], size)]
    width_y = sources[0].shape[1]
    planes = GROUP + 2 * HALO
    step = STEP if count % STEP == 0 else STEP // 2
    cells = GROUP * width_y * width_z
    out_shape = [jax.ShapeDtypeStruct((count, cells), jnp.bfloat16)]
    if cond is None:
        out_shape += [jax.ShapeDtypeStruct((planes, width_y, width_z), jnp.float32)]
    field = pltpu.VMEM((planes, width_y, step, width_z), jnp.float32)
    scratch = [
        pltpu.VMEM((GROUP, width_y, width_z), jnp.float32),
        pltpu.VMEM((planes, step * width_y, width_z), jnp.float32),
        field,
        field,
        field,
        pltpu.VMEM((width_y, step, width_z), jnp.float32),
    ]
    operands = [place, *sources, shift, band] + ([] if cond is None else [cond])
    return call(
        functools.partial(sweep_kernel, adjoint, layout, begin, shift.shape[0] if cond is None else None),
        "adjoint_sweeps" if adjoint else "direct_sweeps",
        [SCALAR] + [FAST] * (len(operands) - 1),
        out_shape,
        scratch,
        SWEEP_COST * count * cells,
        *operands,
    )


def scaled_factors(factors, singular):
    return (factors * (1.0 / jnp.sqrt(singular[...]))).astype(jnp.bfloat16)


def slab(refs, at, depth):
    span = pl.ds(pl.multiple_of(at, 128), depth)
    return jnp.concatenate([ref[:, span] for ref in refs], axis=0)


def gram_kernel(start, chunks, parts, shares, last, info, factors, singular, *refs):
    own, far, direct = refs[:chunks], refs[chunks : 2 * chunks], refs[2 * chunks : 2 * chunks + parts]
    rest = refs[2 * chunks + parts :]
    if last:
        older, older_modes = rest[:2]
        rest = rest[2:]
        kept, sent, kept_modes, sent_modes = rest[0], rest[1:-4], rest[-4], rest[-3]
    pieces, modes = rest[-2:]
    member, core, share = info[0], info[1], info[2]
    adjoint = [ref for pair in zip(own, far) for ref in pair]
    rows_total, cells = sum(ref.shape[0] for ref in adjoint), own[0].shape[1]
    count, width, _ = pieces.shape
    depth = cells // GROUP
    dims = (((1,), (1,)), ((), ()))
    flip = rows_total > count * width
    total = jnp.zeros((rows_total, count * width) if flip else (count * width, rows_total), jnp.float32)
    for plane in range(GROUP):
        rows, cols = slab(adjoint, plane * depth, depth), slab(direct, plane * depth, depth)
        pair = (rows, cols) if flip else (cols, rows)
        total = total + lax.dot_general(*pair, dims, preferred_element_type=jnp.float32)
    if flip:
        total = total.T
    per_share = factors.shape[1] // shares
    window = factors[:, pl.ds(pl.multiple_of(share * per_share, per_share), per_share)]
    window = scaled_factors(window[:, start : start + rows_total], singular)

    def by_half(mine, other):
        return [jnp.where(core == 0, mine, other), jnp.where(core == 0, other, mine)]

    left, ordered, at = [], [], 0
    for ref in own:
        middle, end = at + ref.shape[0], at + 2 * ref.shape[0]
        left += by_half(window[:, at:middle], window[:, middle:end])
        ordered += by_half(total[:, at:middle], total[:, middle:end])
        at = end
    ordered = jnp.concatenate(ordered, axis=1)
    for part in range(count):
        pieces[part] = ordered[part * width : (part + 1) * width]
    term = jnp.dot(
        jnp.concatenate(left, axis=1), slab(adjoint, member * depth, depth), preferred_element_type=jnp.float32
    )
    if not last:
        modes[...] = term
        return
    modes[...] = older_modes[...] + term
    for number in range(len(sent) + 1):
        index = info[4 + number]
        if number == 0:
            kept[:, 0:start] = older[index]
            kept[:, start:] = pieces[index]
        else:
            sent[number - 1][:, 0:start] = older[index].astype(jnp.bfloat16)
            sent[number - 1][:, start:] = pieces[index].astype(jnp.bfloat16)
    wide = depth // shares
    for step in range(shares):
        piece = modes[:, pl.ds(pl.multiple_of(((share + step) % shares) * wide, wide), wide)]
        if step == 0:
            kept_modes[...] = piece
        else:
            sent_modes[step - 1] = piece.astype(jnp.bfloat16)


def gram_part(info, start, own, far, factors, singular, direct, blocks, older, layers):
    cells = own[0].shape[1]
    width = direct[0].shape[0]
    shares = len(direct) // blocks
    mode_count, rows = factors.shape[0], factors.shape[1] // shares
    depth = cells // GROUP
    height = 2 * sum(a.shape[0] for a in own)
    pieces = (shares * blocks, width, height)
    operands = [info, factors, singular, *own, *far, *direct]
    if older is None:
        out_shape = [
            jax.ShapeDtypeStruct(pieces, jnp.float32),
            jax.ShapeDtypeStruct((mode_count, depth), jnp.float32),
        ]
        scratch = []
    else:
        operands += older
        out_shape = [jax.ShapeDtypeStruct((width, rows), jnp.float32)]
        out_shape += [jax.ShapeDtypeStruct((width, rows), jnp.bfloat16)] * (layers - 1)
        out_shape += [
            jax.ShapeDtypeStruct((mode_count, depth // shares), jnp.float32),
            jax.ShapeDtypeStruct((shares - 1, mode_count, depth // shares), jnp.bfloat16),
        ]
        scratch = [pltpu.VMEM(pieces, jnp.float32), pltpu.VMEM((mode_count, depth), jnp.float32)]
    return call(
        functools.partial(gram_kernel, start, len(own), len(direct), shares, older is not None),
        "gram_part",
        [SCALAR] + [FAST] * (len(operands) - 1),
        out_shape,
        scratch,
        height * cells,
        *operands,
    )


def modes_kernel(parts, shares, info, factors, singular, *refs):
    direct, kept, sent = refs[:parts], refs[parts], refs[parts + 1 :]
    member, share = info[0], info[2]
    depth = direct[0].shape[1] // GROUP
    wide = depth // shares
    width = direct[0].shape[0]
    blocks = parts // shares

    def columns(owner, number):
        base = (owner * blocks + number) * GROUP * width
        spans = [factors[:, base + i * width : base + (i + 1) * width] for i in range(GROUP)]
        return sum(jnp.where(member == i, span, 0.0) for i, span in enumerate(spans))

    right = []
    for part in range(parts):
        owner = (share + shares - part // blocks) % shares
        right.append(sum(jnp.where(owner == i, columns(i, part % blocks), 0.0) for i in range(shares)))
    right = scaled_factors(jnp.concatenate(right, axis=1), singular)
    for mask in range(GROUP):
        at = (member ^ mask) * depth + share * wide
        term = jnp.dot(right, slab(direct, at, wide), preferred_element_type=jnp.float32)
        if mask == 0:
            kept[...] = term
        else:
            sent[mask - 1][...] = term.astype(jnp.bfloat16)


def direct_part(info, factors, singular, direct, shares):
    width, cells = direct[0].shape
    shape = (factors.shape[0], cells // GROUP // shares)
    operands = [info, factors, singular, *direct]
    return call(
        functools.partial(modes_kernel, len(direct), shares),
        "direct_modes_part",
        [SCALAR] + [FAST] * (len(operands) - 1),
        [jax.ShapeDtypeStruct(shape, jnp.float32)] + [jax.ShapeDtypeStruct(shape, jnp.bfloat16)] * (GROUP - 1),
        [],
        width * cells,
        *operands,
    )


def band_matrix(width):
    near = (jnp.abs(jnp.arange(width)[:, None] - jnp.arange(width)[None, :]) == 1).astype(jnp.bfloat16)
    return jnp.concatenate([near, near])


def lookup(indices, shift_list):
    levels = jnp.arange(shift_list.shape[0], dtype=jnp.int32)
    picked = jnp.where(indices[:, None] == levels[None, :], shift_list[None, :], jnp.float32(0.0))
    return jnp.sum(picked, axis=1)


def pick(array, index, axis=0):
    return lax.dynamic_index_in_dim(array, index, axis, keepdims=False)


def after(array, *others):
    return lax.optimization_barrier((array, *others))[0]


def per_device(
    forcing_direct,
    forcing_adjoint,
    conductance,
    shift_table,
    freq_direct,
    freq_adjoint,
    left_factors,
    right_factors,
    singular_values,
):
    n_space, n_snap = lax.axis_size("space"), lax.axis_size("snap")
    rows, plane_x, width_y, width_z = forcing_direct.shape
    layers = n_space // GROUP
    block = rows * n_snap // n_space
    blocks = rows // (GROUP * block)
    mode_count = left_factors.shape[1]
    rows_y = width_y // n_snap
    weight = 1.0 / math.sqrt(plane_x * n_space * width_y * width_z)

    spot, share = lax.axis_index("space"), lax.axis_index("snap")
    layer, member = spot // GROUP, spot % GROUP
    core, high = member % 2, member // 2

    def piece_index(target):
        return ((share - target // blocks) % n_snap) * blocks + target % blocks

    info = jnp.stack(
        [member, core, share, layer] + [piece_index((layer + step) % layers) for step in range(layers)]
    ).astype(jnp.int32)

    def swap(array, mask):
        return lax.ppermute(array, "space", [(i, i ^ mask) for i in range(n_space)])

    def around(array, step):
        return lax.ppermute(array, "snap", [(i, (i + step) % n_snap) for i in range(n_snap)])

    ups = [(i, i + GROUP) for i in range(n_space - GROUP)]
    downs = [(i + GROUP, i) for i in range(n_space - GROUP)]
    upper = lambda pairs, wanted: [p for p in pairs if (p[0] % GROUP) // 2 == wanted]
    early = lambda array: lax.ppermute(array, "space", upper(ups, 1) + upper(downs, 0))
    late = lambda array: lax.ppermute(array, "space", upper(ups, 0) + upper(downs, 1))

    sizes = [rows * part // sum(CHUNKS) // 32 * 16 for part in CHUNKS[1:]]
    sizes = [rows // 2 - sum(sizes)] + sizes
    starts = [2 * sum(sizes[:i]) for i in range(len(sizes))]
    sets = forcing_direct.reshape(blocks, GROUP, block, width_y, width_z)
    rows_adj = forcing_adjoint.reshape(rows, width_y, width_z)
    own = lambda i: ("half", starts[i], sizes[i], False)
    cross = lambda i: ("half", starts[i], sizes[i], True)
    near_d, far_d, cross_d, own_d = pack(info, sets, conductance, info, [[("set", mask)] for mask in (2, 3, 1, 0)])
    crossed_d = swap(cross_d, 1)
    to_core, *own_adj = pack(
        info,
        rows_adj,
        conductance,
        crossed_d,
        [[cross(i) for i in range(len(sizes))]] + [[own(i)] for i in range(len(sizes))],
    )

    wide = lambda values: jnp.broadcast_to(values[:, None], (values.shape[0], width_z))
    dir_levels = lookup(freq_direct, shift_table).reshape(blocks, GROUP, block)
    dir_shift = wide(pick(dir_levels, member, 1).reshape(-1))
    adj_levels = lookup(freq_adjoint, shift_table)
    adj_shift = [
        wide(lax.dynamic_slice_in_dim(adj_levels, at + core * size, size, 0)) for at, size in zip(starts, sizes)
    ]
    inside = lambda index: HALO + index
    below = lambda index: index - HALO
    above = lambda index: index + GROUP + HALO
    place = jnp.stack(
        [inside(member ^ k) for k in range(4)]
        + [jnp.where(high == 1, below(member ^ k), above(member ^ k)) for k in (0, 1)]
        + [jnp.where(high == 1, above(member ^ k), below(member ^ k)) for k in (2, 3)]
    ).astype(jnp.int32)
    band = band_matrix(width_z)

    near, far = swap(near_d, 2), swap(far_d, 3)
    crossed = swap(to_core, 1)
    pair_d = join(own_d, crossed_d, 0)
    spots = [sum(sizes[:i]) for i in range(len(sizes))]
    pairs = [join(own, crossed, at) for own, at in zip(own_adj, spots)]
    e_d = early(pair_d)
    late_near, late_far = late(near), late(far)
    sources = [pair_d, near, far, e_d, late_near, late_far]
    dir_state, cond = sweep(False, place, sources, dir_shift, band, None, (0, block))
    dir_states = [dir_state] + [
        sweep(False, place, sources, dir_shift, band, cond, (i * block, block))[0] for i in range(1, blocks)
    ]
    moved = [[around(state, step) for state in dir_states] for step in range(1, n_snap)]
    everyone = dir_states + [state for states in moved for state in states]
    singular = singular_values.reshape(1, mode_count).T
    left, right = left_factors.T, right_factors.T
    kept, *sent = direct_part(info, right, singular, everyone, n_snap)
    y_adj, e_adj, l_adj, own_states, far_states = [], [], [], [], []
    for i, pair in enumerate(pairs):
        y_after = [near, far, late_near] if i == 0 else [y_adj[-1], dir_states[0]]
        e_after = [e_d] if i == 0 else [e_adj[-1], dir_states[-1] if i == 1 else y_adj[1]]
        y_adj.append(swap(after(pair, *y_after), 2))
        e_adj.append(early(after(pair, *e_after)))
        l_adj.append(late(after(y_adj[i], l_adj[-1]) if i else y_adj[i]))
        arrived = after(y_adj[i], everyone[blocks]) if i == 1 else y_adj[i]
        if i == 2:
            arrived = after(y_adj[i], kept)
        sources = [pair, arrived, e_adj[i], l_adj[i]]
        own_states.append(sweep(True, place, sources, adj_shift[i], band, cond)[0])
        far_states.append(swap(own_states[i], 1))

    for mask in range(1, GROUP):
        kept = kept + swap(sent[mask - 1], mask).astype(jnp.float32)
    direct_modes = kept.reshape(mode_count, 1, rows_y, width_z)

    outs = gram_part(
        info, 0, own_states[:-1], far_states[:-1], left, singular, everyone, blocks, None, layers
    )
    outs = gram_part(
        info, starts[-1], own_states[-1:], far_states[-1:], left, singular, everyone, blocks, list(outs), layers
    )
    kept, *sent, kept_modes, sent_modes = outs
    for step in range(1, layers):
        pairs = [(i, (i + GROUP * step) % n_space) for i in range(n_space)]
        kept = kept + lax.ppermute(sent[step - 1], "space", pairs).astype(jnp.float32)
    gram = (kept * weight).T
    for step in range(1, n_snap):
        kept_modes = kept_modes + around(sent_modes[step - 1], step).astype(jnp.float32)
    adjoint_modes = kept_modes.reshape(mode_count, 1, rows_y, width_z)
    return (gram, direct_modes, adjoint_modes)


def solution(mesh):
    placed = (
        P("snap", "space", None, None),
        P("snap", "space", None, None),
        P("space", None, None),
        P(),
        P("snap"),
        P("snap"),
        P(),
        P(),
        P(),
    )
    return jax.shard_map(
        per_device,
        mesh=mesh,
        in_specs=placed,
        out_specs=(
            P("snap", "space"),
            P(None, "space", "snap", None),
            P(None, "space", "snap", None),
        ),
        check_vma=False,
    )
```
